512 devices in a mesh: seq: 32 (over x_hi, z), lat: 16 (over x_lo, y, core).
Axes of the slice: x: 4 (x_hi: 2, x_lo: 2; x = x_hi * 2 + x_lo), y: 4, z: 16, core: 2. Of those that a mesh axis runs over, the one named last changes fastest.
Arguments:
- inputs: bfloat16 [24576, 2048], P('seq'), may hold values from -6 to 6
- cross_kv: bfloat16 [2048, 2, 2048], P(None, None, 'lat'), may hold values from -0.125 to 0.125
- cross_out_w: bfloat16 [2048, 2048], P('lat'), may hold values from -0.5 to 0.5
- latent_query: bfloat16 [1024, 2048], P('seq', 'lat')
- latent_base: bfloat16 [1024, 2048], P('seq'), may hold values from -1.75 to 1.75
- latent_pos: int32 [1024], replicated, may hold values from 0 to 24575, as said below
- attn_qkv: bfloat16 [1, 2048, 3, 2048], P(None, 'seq', None, 'lat'), may hold values from -0.125 to 0.125
- attn_out: bfloat16 [1, 2048, 2048], P(None, 'seq', 'lat'), may hold values from -2 to 2
- mlp_up: bfloat16 [1, 2048, 8192], P(None, 'seq', 'lat'), may hold values from -0.125 to 0.125
- mlp_down: bfloat16 [1, 2048, 8192], P(None, 'seq', 'lat'), may hold values from -0.0625 to 0.0625
Outputs:
- latent_out: bfloat16 [1024, 2048], P(('seq', 'lat'))
The draws below stay inside these ranges and needn't reach their ends.
Inputs may be any that keep to these rules, and one draw needn't show every extreme that they name: `latent_pos`: strictly increasing along the latents; the last latent sits at position 24575.
All inputs are finite; a program needn't handle non-finite values.
Results may differ from the reference program's by a relative error of at most 0.025.
Values may be sent and summed in bfloat16 or wider, within the bound.
A program may use at most 64 MiB of HBM per device.

```python
import math
import jax
import jax.numpy as jnp
from jax import lax

HD = 128
HEADS = 16
D = 2048
FF = 8192
LATENTS = 1024
SEQ = 24576
LAYERS = 1


def draw_latent_pos(key, part):
    key = jax.random.fold_in(key, 11)
    gap_most = (SEQ - 1) // (LATENTS - 1)
    gaps = jax.random.randint(key, (LATENTS - 1,), 1, gap_most + 1, dtype=jnp.int32)
    suffix = jnp.cumsum(gaps[::-1])[::-1]
    last = jnp.full((1,), SEQ - 1, dtype=jnp.int32)
    return jnp.concatenate([(SEQ - 1 - suffix).astype(jnp.int32), last])


def draw_latent_query(key, part):
    key = jax.random.fold_in(key, 5)
    values = jnp.clip(jax.random.normal(key, (LATENTS, D), jnp.float32) * 2.0, -12.0, 12.0)
    return values.astype(jnp.bfloat16)


def block_levels(rng, shape, cuts, least, top_value):
    gain, own = 1.0, jax.random.fold_in(rng, 6)
    for dim, shards_of in cuts:
        draws = jnp.exp(jax.random.uniform(jax.random.fold_in(own, dim), (shards_of,), jnp.float32, least / len(cuts), top_value / len(cuts)))
        gain = gain * jnp.repeat(draws, shape[dim] // shards_of).reshape([-1 if axis == dim else 1 for axis in range(len(shape))])
    return gain


def normal_values(rng, extent, spread, most, shards=(), held_as=jnp.bfloat16):
    array = jax.random.normal(rng, extent, jnp.float32) * spread
    if len(shards) > 0:
        array = block_levels(rng, extent, shards, -0.22, 0.18) * array
    return jnp.clip(array, min=-most, max=most).astype(held_as)


def setup_inputs(seed: int = 0) -> dict:
    streams_of = jax.random.split(jax.random.key(seed), 11)
    inputs = normal_values(streams_of[0], (SEQ, D), 1.0, 6.0, ((0, 32),))
    cross_kv = normal_values(streams_of[1], (D, 2, D), D ** -0.5, 0.125, ((2, 16),))
    cross_out_w = normal_values(streams_of[2], (D, D), HD ** -0.5, 0.5, ((0, 16),))
    latent_query = draw_latent_query(jax.random.fold_in(streams_of[10], 71), 0)
    latent_base = normal_values(streams_of[4], (LATENTS, D), 0.3, 1.75, ((0, 32),))
    latent_pos = draw_latent_pos(jax.random.fold_in(streams_of[10], 71), 0)
    attn_qkv = normal_values(streams_of[6], (LAYERS, D, 3, D), D ** -0.5, 0.125, ((1, 32), (3, 16)))
    attn_out = normal_values(streams_of[7], (LAYERS, D, D), (max(HD // 16, 1)) ** -0.5, 2.0, ((1, 32), (2, 16)))
    mlp_up = normal_values(streams_of[8], (LAYERS, D, FF), D ** -0.5, 0.125, ((1, 32), (2, 16)))
    mlp_down = normal_values(streams_of[9], (LAYERS, D, FF), FF ** -0.5, 0.0625, ((1, 32), (2, 16)))
    return dict(inputs=inputs, cross_kv=cross_kv, cross_out_w=cross_out_w, latent_query=latent_query, latent_base=latent_base, latent_pos=latent_pos, attn_qkv=attn_qkv, attn_out=attn_out, mlp_up=mlp_up, mlp_down=mlp_down)


def rms(h):
    return h * lax.rsqrt(lax.optimization_barrier(jnp.mean(h * h, axis=-1, keepdims=True)) + 1e-06)

def reference(inputs, cross_kv, cross_out_w, latent_query, latent_base, latent_pos, attn_qkv, attn_out, mlp_up, mlp_down):
    scale = 1.0 / math.sqrt(HD)
    kv = jnp.einsum('td,dch->tch', inputs.astype(jnp.float32), cross_kv.astype(jnp.float32)).astype(jnp.bfloat16)
    keyvals = kv.reshape(SEQ, 2, HEADS, HD).transpose(2, 0, 1, 3)
    queries = latent_query.reshape(LATENTS, HEADS, HD).transpose(1, 0, 2)
    allowed = jnp.arange(SEQ, dtype=jnp.int32)[None, :] <= latent_pos[:, None]

    def cross_head(pair):
        query, keyval = pair
        scores = jnp.dot(query, keyval[:, 0].T, preferred_element_type=jnp.float32) * scale
        masked = jnp.where(allowed, scores, -1e+30)
        top = lax.optimization_barrier(jnp.max(masked, axis=1, keepdims=True))
        weights = jnp.where(allowed, jnp.exp(scores - top), 0.0)
        total = lax.optimization_barrier(jnp.sum(weights, axis=1, keepdims=True))
        numer = jnp.dot(weights.astype(jnp.bfloat16), keyval[:, 1], preferred_element_type=jnp.float32)
        return (numer / total).astype(jnp.bfloat16)
    context = lax.map(cross_head, (queries, keyvals))
    context = context.transpose(1, 0, 2).reshape(LATENTS, D)
    h = latent_base.astype(jnp.float32) + jnp.dot(context, cross_out_w, preferred_element_type=jnp.float32)
    index = jnp.arange(LATENTS, dtype=jnp.int32)
    causal = index[None, :] <= index[:, None]

    def self_head(part):
        raw = jnp.dot(part[:, 0], part[:, 1].T, preferred_element_type=jnp.float32) * scale
        capped = 30.0 * jnp.tanh(raw / 30.0)
        expo = jnp.where(causal, jnp.exp(capped), 0.0)
        total = lax.optimization_barrier(jnp.sum(expo, axis=1, keepdims=True))
        numer = jnp.dot(expo.astype(jnp.bfloat16), part[:, 2], preferred_element_type=jnp.float32)
        return (numer / total).astype(jnp.bfloat16)
    for layer in range(LAYERS):
        normed = rms(h).astype(jnp.bfloat16)
        qkv = jnp.einsum('ld,dch->lch', normed.astype(jnp.float32), attn_qkv[layer].astype(jnp.float32)).astype(jnp.bfloat16)
        parts = qkv.reshape(LATENTS, 3, HEADS, HD).transpose(2, 0, 1, 3)
        self_context = lax.map(self_head, parts).transpose(1, 0, 2).reshape(LATENTS, D)
        h = h + jnp.dot(self_context, attn_out[layer].T, preferred_element_type=jnp.float32)
        normed2 = rms(h).astype(jnp.bfloat16)
        hidden = jax.nn.gelu(jnp.dot(normed2, mlp_up[layer], preferred_element_type=jnp.float32)).astype(jnp.bfloat16)
        h = h + jnp.dot(hidden, mlp_down[layer].T, preferred_element_type=jnp.float32)
    return h.astype(jnp.bfloat16)
```

```python
import math

import jax
import jax.numpy as jnp
from jax import lax
from jax.experimental import pallas as pl
from jax.experimental.pallas import tpu as pltpu
from jax.sharding import PartitionSpec as P

HD = 128
NSEQ = 32
NZ = 16
NLAT = 16
ROWS = 32
LATENTS = 1024
TOK = 768
D = 2048
HID = 512
CHUNK = 64
MESH = pl.DeviceIdType.MESH
F32 = jnp.float32
BF16 = jnp.bfloat16
LOG2E = 1.4426950408889634
SCALE = 1.0 / math.sqrt(HD)
LOW = -1e30


def dot_nt(a, b):
    return lax.dot_general(a, b, (((1,), (1,)), ((), ())), preferred_element_type=F32)


def dot_nn(a, b):
    return jnp.dot(a, b, preferred_element_type=F32)


def kernel(
    x_hbm,
    ckv_hbm,
    wo_ref,
    q_ref,
    base_ref,
    pos_ref,
    w0_ref,
    w1_ref,
    w2_ref,
    out_ref,
    xv,
    ckvv,
    keys,
    vals,
    qbuf,
    wbuf,
    csend,
    crecv,
    lsend,
    lrecv,
    lmat,
    ltr,
    rsend,
    rrecv,
    hsend,
    gath,
    kvbuf,
    part,
    fsend,
    frecv,
    load_sem,
    qs_sem,
    qr_sem,
    ws_sem,
    wf_sem,
    wb_sem,
    wx_sem,
    cs_sem,
    cr_sem,
    ls_sem,
    lr_sem,
    rs_sem,
    rr_sem,
    gs_sem,
    gr_sem,
    ks_sem,
    kr_sem,
    fs_sem,
    fr_sem,
):
    me = lax.axis_index("seq")
    lme = lax.axis_index("lat")
    xh = me // NZ
    z = lax.rem(me, NZ)
    partner = lax.rem(me + NZ, NSEQ)
    z_up = xh * NZ + lax.rem(z + 1, NZ)
    z_down = xh * NZ + lax.rem(z + NZ - 1, NZ)
    my_quad = me // 4

    load_x = pltpu.make_async_copy(x_hbm, xv, load_sem.at[0])
    load_kv = pltpu.make_async_copy(ckv_hbm, ckvv, load_sem.at[1])
    load_x.start()
    load_kv.start()

    kvbuf[...] = jnp.zeros_like(kvbuf)

    barrier = pltpu.get_barrier_semaphore()

    def greet_seq(i, carry):
        pl.semaphore_signal(
            barrier,
            inc=1,
            device_id={"seq": lax.rem(me + i, NSEQ)},
            device_id_type=MESH,
        )
        return carry

    def greet_lat(i, carry):
        pl.semaphore_signal(
            barrier,
            inc=1,
            device_id={"lat": lax.rem(lme + i, NLAT)},
            device_id_type=MESH,
        )
        return carry

    lax.fori_loop(1, NSEQ, greet_seq, 0)
    lax.fori_loop(1, NLAT, greet_lat, 0)

    qbuf[me] = q_ref[...]
    wbuf[0, me] = w0_ref[...]
    wbuf[1, me] = w1_ref[...]
    wbuf[2, me] = w2_ref[...]

    pl.semaphore_wait(barrier, NSEQ - 1 + NLAT - 1)

    def drain(ref, sem):
        pltpu.make_async_copy(ref, ref, sem).wait()

    def send_query(i, carry):
        p = lax.rem(me + i, NSEQ)
        pltpu.make_async_remote_copy(
            src_ref=qbuf.at[me],
            dst_ref=qbuf.at[me],
            send_sem=qs_sem,
            recv_sem=qr_sem.at[my_quad],
            device_id={"seq": p},
            device_id_type=MESH,
        ).start()
        return carry

    lax.fori_loop(1, NSEQ, send_query, 0)

    def move(r, src, to, recv_sem):
        return pltpu.make_async_remote_copy(
            src_ref=wbuf.at[r, src],
            dst_ref=wbuf.at[r, src],
            send_sem=ws_sem.at[r],
            recv_sem=recv_sem,
            device_id={"seq": to},
            device_id_type=MESH,
        )

    def from_below(k):
        return xh * NZ + lax.rem(z + NZ - k, NZ)

    def from_above(k):
        return xh * NZ + lax.rem(z + k, NZ)

    def ring_start(r):
        move(r, me, z_up, wf_sem.at[r, 1]).start()
        move(r, me, z_down, wb_sem.at[r, 1]).start()
        move(r, me, partner, wx_sem.at[r]).start()

    def ring_step(r, k):
        low = from_below(k)
        move(r, low, z_up, wf_sem.at[r, k]).wait_recv()

        @pl.when(k < 8)
        def _():
            move(r, low, z_up, wf_sem.at[r, k + 1]).start()

        move(r, low, partner, wx_sem.at[r]).start()

        @pl.when(k < 8)
        def _():
            high = from_above(k)
            move(r, high, z_down, wb_sem.at[r, k]).wait_recv()

            @pl.when(k < 7)
            def _():
                move(r, high, z_down, wb_sem.at[r, k + 1]).start()

            move(r, high, partner, wx_sem.at[r]).start()

    def ring_steps(r, first, last):
        def body(k, carry):
            ring_step(r, k)
            return carry

        lax.fori_loop(first, last + 1, body, 0)

    def ring_finish(r):
        other = (1 - xh) * NZ
        drain(wbuf.at[r, pl.ds(other, NZ)], wx_sem.at[r])

    def ring_sent(r):
        drain(wbuf.at[r, pl.ds(0, 31)], ws_sem.at[r])

    ring_start(0)

    load_kv.wait()
    load_x.wait()
    for half in range(2):
        rows = pl.ds(half * (TOK // 2), TOK // 2)
        kv = dot_nn(xv[rows, :], ckvv[...])
        keys[rows, :] = kv[:, :HD].astype(BF16)
        vals[rows, :] = kv[:, HD:].astype(BF16)

    key_pos = me * TOK + lax.broadcasted_iota(jnp.int32, (1, TOK), 1)

    def quad_step(j, carry):
        quad = lax.rem(my_quad + j, 8)

        @pl.when(j == 0)
        def _():
            drain(qbuf.at[pl.ds(0, 3)], qr_sem.at[quad])

        @pl.when(j > 0)
        def _():
            drain(qbuf.at[pl.ds(0, 4)], qr_sem.at[quad])

        q = qbuf[pl.ds(quad * 4, 4)].reshape(4 * ROWS, HD)
        scores = dot_nt(q, keys[...])
        pos = pos_ref[pl.ds(pl.multiple_of(quad * 128, 128), 128), :]
        allowed = key_pos <= pos
        top = jnp.max(jnp.where(allowed, scores, LOW), axis=1, keepdims=True)
        weights = jnp.where(allowed, jnp.exp2((scores - top) * (SCALE * LOG2E)), 0.0)
        total = jnp.sum(weights, axis=1, keepdims=True)
        numer = dot_nn(weights.astype(BF16), vals[...])
        some = total > 0.0
        ctx = numer / jnp.where(some, total, 1.0)
        lse = jnp.where(some, top * (SCALE * LOG2E) + jnp.log2(jnp.where(some, total, 1.0)), LOW)
        csend[pl.ds(quad * 4, 4)] = ctx.astype(BF16).reshape(4, ROWS, HD)
        lsend[quad] = jnp.broadcast_to(lse, (128, 128)).T[0:1, :]

        def send_part(t, carry):
            p = quad * 4 + t

            @pl.when(p != me)
            def _():
                pltpu.make_async_remote_copy(
                    src_ref=csend.at[p],
                    dst_ref=crecv.at[me],
                    send_sem=cs_sem,
                    recv_sem=cr_sem,
                    device_id={"seq": p},
                    device_id_type=MESH,
                ).start()
                pltpu.make_async_remote_copy(
                    src_ref=lsend.at[quad],
                    dst_ref=lrecv.at[me],
                    send_sem=ls_sem,
                    recv_sem=lr_sem,
                    device_id={"seq": p},
                    device_id_type=MESH,
                ).start()

            return carry

        lax.fori_loop(0, 4, send_part, 0)
        ring_step(0, j + 1)
        return carry

    lax.fori_loop(0, 8, quad_step, 0)

    crecv[me] = csend[me]
    lrecv[me] = lsend[my_quad]
    ring_start(1)
    drain(qbuf.at[pl.ds(0, 31)], qs_sem)
    ring_steps(1, 1, 4)
    drain(crecv.at[pl.ds(0, 31)], cr_sem)
    drain(lrecv.at[pl.ds(0, 31)], lr_sem)

    for s in range(NSEQ):
        lmat[s : s + 1, :] = lrecv[s]
    logs = lmat[0:NSEQ, :]
    share = jnp.exp2(logs - jnp.max(logs, axis=0, keepdims=True))
    lmat[0:NSEQ, :] = share / jnp.sum(share, axis=0, keepdims=True)
    lmat[NSEQ:, :] = jnp.zeros((128 - NSEQ, 128), F32)
    ltr[...] = lmat[...].T
    mine = ltr[pl.ds(pl.multiple_of(lax.rem(me, 4) * ROWS, ROWS), ROWS), :]
    context = jnp.zeros((ROWS, HD), F32)
    for s in range(NSEQ):
        context += mine[:, s : s + 1] * crecv[s].astype(F32)

    def scatter_start(n, term):
        for f in range(NLAT):
            rsend[n, f] = term[:, f * HD : (f + 1) * HD].astype(BF16)

        def send(i, carry):
            p = lax.rem(lme + i, NLAT)
            pltpu.make_async_remote_copy(
                src_ref=rsend.at[n, p],
                dst_ref=rrecv.at[n, i],
                send_sem=rs_sem.at[n],
                recv_sem=rr_sem.at[n],
                device_id={"lat": p},
                device_id_type=MESH,
            ).start()
            return carry

        lax.fori_loop(1, NLAT, send, 0)

    def scatter_finish(n):
        drain(rrecv.at[n, pl.ds(1, NLAT - 1)], rr_sem.at[n])
        acc = rsend[n, lme].astype(F32)
        for i in range(1, NLAT):
            acc += rrecv[n, i].astype(F32)
        return acc

    def gather_start(n, h):
        hsend[n] = h.astype(BF16)
        gath[n, lme] = h.astype(BF16)

        def send(i, carry):
            pltpu.make_async_remote_copy(
                src_ref=hsend.at[n],
                dst_ref=gath.at[n, lme],
                send_sem=gs_sem.at[n],
                recv_sem=gr_sem.at[n],
                device_id={"lat": lax.rem(lme + i, NLAT)},
                device_id_type=MESH,
            ).start()
            return carry

        lax.fori_loop(1, NLAT, send, 0)

    def gather_finish(n):
        drain(gath.at[n, pl.ds(0, NLAT - 1)], gr_sem.at[n])
        rows = jnp.concatenate([gath[n, f] for f in range(NLAT)], axis=1)
        wide = rows.astype(F32)
        gain = lax.rsqrt(jnp.mean(wide * wide, axis=-1, keepdims=True) + 1e-06)
        return rows, gain

    def weight(r):
        return wbuf[r].reshape(D, HID)

    my_cols = pl.ds(pl.multiple_of(lme * HD, HD), HD)
    scatter_start(0, dot_nn(context.astype(BF16), wo_ref[...]))
    ring_sent(0)
    ring_steps(1, 5, 5)
    h = base_ref[:, my_cols].astype(F32) + scatter_finish(0)
    gather_start(0, h)
    ring_steps(1, 6, 6)
    ring_finish(0)
    rows, gain = gather_finish(0)
    qkv = (dot_nn(rows, wbuf[0, :, :, : 3 * HD].reshape(D, 3 * HD)) * gain).astype(BF16)
    query = qkv[:, :HD]
    kvbuf[me] = qkv[:, HD:]

    def kv_copy(source, p):
        return pltpu.make_async_remote_copy(
            src_ref=kvbuf.at[source],
            dst_ref=kvbuf.at[source],
            send_sem=ks_sem.at[p],
            recv_sem=kr_sem.at[source],
            device_id={"seq": p},
            device_id_type=MESH,
        )

    def kv_send(p, carry):
        kv_copy(me, p).start()
        return carry

    def kv_recv(p, carry):
        kv_copy(p, partner).wait_recv()
        return carry

    def kv_sent(p, carry):
        kv_copy(me, p).wait_send()
        return carry

    lax.fori_loop(me + 1, NSEQ, kv_send, 0)
    ring_steps(1, 7, 8)
    ring_start(2)
    drain(crecv.at[pl.ds(0, 31)], cs_sem)
    drain(lrecv.at[pl.ds(0, 31)], ls_sem)
    ring_steps(2, 1, 4)
    lax.fori_loop(0, me, kv_recv, 0)

    kv = kvbuf[...].reshape(LATENTS, 2 * HD)
    raw = dot_nt(query, kv[:, :HD]) * SCALE
    capped = 30.0 * jnp.tanh(raw / 30.0)
    key_row = lax.broadcasted_iota(jnp.int32, (ROWS, LATENTS), 1)
    my_row = me * ROWS + lax.broadcasted_iota(jnp.int32, (ROWS, LATENTS), 0)
    expo = jnp.where(key_row <= my_row, jnp.exp(capped), 0.0)
    self_total = jnp.sum(expo, axis=1, keepdims=True)
    self_ctx = dot_nn(expo.astype(BF16), kv[:, HD:]) / self_total

    scatter_start(1, dot_nt(self_ctx.astype(BF16), wbuf[0, :, :, 3 * HD :].reshape(D, HD)))
    ring_sent(1)
    ring_steps(2, 5, 5)
    h = h + scatter_finish(1)
    gather_start(1, h)
    ring_steps(2, 6, 6)
    ring_finish(1)
    rows, gain = gather_finish(1)
    hidden = jax.nn.gelu(dot_nn(rows, weight(1)) * gain).astype(BF16)
    ring_steps(2, 7, 8)
    ring_finish(2)
    part[...] = dot_nt(hidden, weight(2))
    part[:, my_cols] += h
    for f in range(NLAT):
        fsend[f] = part[2 * f : 2 * f + 2, :]

    def last_send(i, carry):
        p = lax.rem(lme + i, NLAT)
        pltpu.make_async_remote_copy(
            src_ref=fsend.at[p],
            dst_ref=frecv.at[i],
            send_sem=fs_sem,
            recv_sem=fr_sem,
            device_id={"lat": p},
            device_id_type=MESH,
        ).start()
        return carry

    lax.fori_loop(1, NLAT, last_send, 0)
    ring_sent(2)
    for n in range(2):
        drain(rrecv.at[n, pl.ds(1, NLAT - 1)], rs_sem.at[n])
        drain(gath.at[n, pl.ds(0, NLAT - 1)], gs_sem.at[n])
    lax.fori_loop(me + 1, NSEQ, kv_sent, 0)
    drain(frecv.at[pl.ds(1, NLAT - 1)], fr_sem)
    acc = fsend[lme]
    for i in range(1, NLAT):
        acc += frecv[i]
    out_ref[...] = acc.astype(BF16)
    drain(frecv.at[pl.ds(1, NLAT - 1)], fs_sem)


def local(
    inputs,
    cross_kv,
    cross_out_w,
    latent_query,
    latent_base,
    latent_pos,
    attn_qkv,
    attn_out,
    mlp_up,
    mlp_down,
):
    dma = pltpu.SemaphoreType.DMA
    vmem = pl.BlockSpec(memory_space=pltpu.VMEM)
    hbm = pl.BlockSpec(memory_space=pl.ANY)
    w0 = jnp.concatenate([attn_qkv[0].reshape(CHUNK, 3 * HD), attn_out[0]], axis=1)
    return pl.pallas_call(
        kernel,
        out_shape=jax.ShapeDtypeStruct((ROWS // NLAT, D), BF16),
        in_specs=[hbm, hbm] + [vmem] * 7,
        out_specs=vmem,
        scratch_shapes=[
            pltpu.VMEM((TOK, D), BF16),
            pltpu.VMEM((D, 2 * HD), BF16),
            pltpu.VMEM((TOK, HD), BF16),
            pltpu.VMEM((TOK, HD), BF16),
            pltpu.VMEM((NSEQ, ROWS, HD), BF16),
            pltpu.VMEM((3, NSEQ, CHUNK, HID), BF16),
            pltpu.VMEM((NSEQ, ROWS, HD), BF16),
            pltpu.VMEM((NSEQ, ROWS, HD), BF16),
            pltpu.VMEM((8, 1, 128), F32),
            pltpu.VMEM((NSEQ, 1, 128), F32),
            pltpu.VMEM((128, 128), F32),
            pltpu.VMEM((128, 128), F32),
            pltpu.VMEM((2, NLAT, ROWS, HD), BF16),
            pltpu.VMEM((2, NLAT, ROWS, HD), BF16),
            pltpu.VMEM((2, ROWS, HD), BF16),
            pltpu.VMEM((2, NLAT, ROWS, HD), BF16),
            pltpu.VMEM((NSEQ, ROWS, 2 * HD), BF16),
            pltpu.VMEM((ROWS, D), F32),
            pltpu.VMEM((NLAT, 2, D), F32),
            pltpu.VMEM((NLAT, 2, D), F32),
            dma((2,)),
            dma,
            dma((8,)),
            dma((3,)),
            dma((3, 9)),
            dma((3, 9)),
            dma((3,)),
            dma,
            dma,
            dma,
            dma,
            dma((2,)),
            dma((2,)),
            dma((2,)),
            dma((2,)),
            dma((NSEQ,)),
            dma((NSEQ,)),
            dma,
            dma,
        ],
        compiler_params=pltpu.CompilerParams(
            collective_id=0, has_side_effects=True, vmem_limit_bytes=52 << 20
        ),
    )(
        inputs,
        cross_kv.reshape(D, 2 * HD),
        cross_out_w,
        latent_query,
        latent_base,
        latent_pos.reshape(LATENTS, 1),
        w0,
        mlp_up[0],
        mlp_down[0],
    )


def solution(mesh):
    return jax.shard_map(
        local,
        mesh=mesh,
        in_specs=(
            P("seq", None),
            P(None, None, "lat"),
            P("lat", None),
            P("seq", "lat"),
            P("seq", None),
            P(),
            P(None, "seq", None, "lat"),
            P(None, "seq", "lat"),
            P(None, "seq", "lat"),
            P(None, "seq", "lat"),
        ),
        out_specs=P(("seq", "lat"), None),
        check_vma=False,
    )
```

```python
import math

import jax
import jax.numpy as jnp
from jax import lax
from jax.experimental import pallas as pl
from jax.experimental.pallas import tpu as pltpu
from jax.sharding import PartitionSpec as P

HD = 128
NSEQ = 32
NZ = 16
NLAT = 16
ROWS = 32
LATENTS = 1024
TOK = 768
D = 2048
HID = 512
CHUNK = 64
MESH = pl.DeviceIdType.MESH
F32 = jnp.float32
BF16 = jnp.bfloat16
LOG2E = 1.4426950408889634
SCALE = 1.0 / math.sqrt(HD)
LOW = -1e30


def dot_nt(a, b):
    return lax.dot_general(a, b, (((1,), (1,)), ((), ())), preferred_element_type=F32)


def dot_nn(a, b):
    return jnp.dot(a, b, preferred_element_type=F32)


def kernel(
    x_hbm,
    ckv_hbm,
    wo_hbm,
    q_hbm,
    base_hbm,
    pos_hbm,
    qkv_hbm,
    ow_hbm,
    up_hbm,
    down_hbm,
    out_ref,
    xv,
    ckvv,
    wov,
    basev,
    posv,
    kvt,
    qbuf,
    wbuf0,
    wbuf1,
    part_n,
    part_m,
    part_l,
    csend,
    crecv,
    lsend,
    lrecv,
    lmat,
    ltr,
    rsend,
    rrecv,
    hsend,
    gath,
    kvbuf,
    qx,
    sx,
    rx,
    part,
    fsend,
    frecv,
    load_sem,
    qs_sem,
    qr_sem,
    xs_sem,
    xr_sem,
    ws_sem,
    wf_sem,
    wb_sem,
    wx_sem,
    cs_sem,
    cr_sem,
    ls_sem,
    lr_sem,
    rs_sem,
    rr_sem,
    gs_sem,
    gr_sem,
    ks_sem,
    kr_sem,
    ps_sem,
    pr_sem,
    fs_sem,
    fr_sem,
):
    me = lax.axis_index("seq")
    lme = lax.axis_index("lat")
    xh = me // NZ
    z = lax.rem(me, NZ)
    line = xh * NZ
    partner = lax.rem(me + NZ, NSEQ)
    my_quad = z // 4
    z_up = line + lax.rem(z + 1, NZ)
    z_down = line + lax.rem(z + NZ - 1, NZ)

    loads = [
        pltpu.make_async_copy(src, dst, load_sem.at[n])
        for n, (src, dst) in enumerate(
            (
                (q_hbm, qbuf.at[z]),
                (qkv_hbm.at[0], wbuf0.at[me, :, pl.ds(0, HD)]),
                (qkv_hbm.at[1], wbuf0.at[me, :, pl.ds(HD, HD)]),
                (qkv_hbm.at[2], wbuf0.at[me, :, pl.ds(2 * HD, HD)]),
                (ow_hbm, wbuf0.at[me, :, pl.ds(3 * HD, HD)]),
                (ckv_hbm, ckvv),
                (x_hbm, xv),
                (up_hbm, wbuf1.at[me, 0]),
                (down_hbm, wbuf1.at[me, 1]),
                (pos_hbm, posv),
                (wo_hbm, wov),
                (base_hbm, basev),
            )
        )
    ]
    for load in loads:
        load.start()

    qx[1] = jnp.zeros((ROWS, HD), BF16)
    rx[...] = jnp.zeros_like(rx)

    barrier = pltpu.get_barrier_semaphore()

    def greet(device_id):
        pl.semaphore_signal(barrier, inc=1, device_id=device_id, device_id_type=MESH)

    def in_line(i):
        return line + lax.rem(z + i, NZ)

    def in_lat(i):
        return lax.rem(lme + i, NLAT)

    def greet_all(i, carry):
        greet({"seq": in_line(i)})
        greet({"lat": in_lat(i)})
        return carry

    lax.fori_loop(1, NZ, greet_all, 0)
    greet({"seq": partner})
    for load in loads[:5]:
        load.wait()
    pl.semaphore_wait(barrier, NZ - 1 + 1 + NLAT - 1)

    def drain(ref, sem):
        pltpu.make_async_copy(ref, ref, sem).wait()

    def remote(src, dst, send_sem, recv_sem, device_id):
        return pltpu.make_async_remote_copy(
            src_ref=src,
            dst_ref=dst,
            send_sem=send_sem,
            recv_sem=recv_sem,
            device_id=device_id,
            device_id_type=MESH,
        )

    def send_query(i, carry):
        remote(qbuf.at[z], qbuf.at[z], qs_sem, qr_sem.at[my_quad], {"seq": in_line(i)}).start()
        return carry

    lax.fori_loop(1, NZ, send_query, 0)

    wbufs = (wbuf0, wbuf1)

    def move(r, src, to, recv_sem):
        chunk = wbufs[r].at[src]
        return remote(chunk, chunk, ws_sem.at[r], recv_sem, {"seq": to})

    def ring_start(r):
        move(r, me, z_up, wf_sem.at[r, 1]).start()
        move(r, me, z_down, wb_sem.at[r, 1]).start()

    def ring_step(r, k):
        low = line + lax.rem(z + NZ - k, NZ)
        high = line + lax.rem(z + k, NZ)
        move(r, low, z_up, wf_sem.at[r, k]).wait_recv()
        if k < 8:
            move(r, low, z_up, wf_sem.at[r, k + 1]).start()
            move(r, high, z_down, wb_sem.at[r, k]).wait_recv()
            if k < 7:
                move(r, high, z_down, wb_sem.at[r, k + 1]).start()
        move(r, low, partner, wx_sem.at[r]).start()
        if k < 8:
            move(r, high, partner, wx_sem.at[r]).start()

    def ring_finish(r):
        drain(wbufs[r].at[pl.ds((1 - xh) * NZ, NZ)], wx_sem.at[r])

    def ring_sent(r):
        drain(wbufs[r].at[pl.ds(0, 31)], ws_sem.at[r])

    ring_start(0)

    loads[5].wait()
    loads[6].wait()
    half_rows = TOK // 2
    for half in range(2):
        rows = pl.ds(half * half_rows, half_rows)
        kvt[0, rows, :] = dot_nn(xv[rows, :], ckvv[...]).astype(BF16)
        remote(kvt.at[0, rows], kvt.at[1, rows], xs_sem, xr_sem, {"seq": partner}).start()
    move(0, me, partner, wx_sem.at[0]).start()
    for load in loads[7:]:
        load.wait()
    ring_step(0, 1)

    def attend(quad, slot, owner):
        q = qbuf[pl.ds(quad * 4, 4)].reshape(4 * ROWS, HD)
        scores = dot_nt(q, kvt[slot, :, :HD])
        row = posv[pl.ds(xh * 4 + quad, 1), :].astype(F32)
        pos = jnp.broadcast_to(row, (128, 128)).T[:, 0:1]
        key = lax.broadcasted_iota(jnp.int32, (1, TOK), 1) + owner * TOK
        allowed = key.astype(F32) <= pos
        top = jnp.max(jnp.where(allowed, scores, LOW), axis=1, keepdims=True)
        weights = jnp.where(allowed, jnp.exp2((scores - top) * (SCALE * LOG2E)), 0.0)
        total = jnp.sum(weights, axis=1, keepdims=True)
        numer = dot_nn(weights.astype(BF16), kvt[slot, :, HD:])
        return top, total, numer

    def first_pass(j, carry):
        quad = lax.rem(my_quad + j, 4)

        @pl.when(j == 0)
        def _():
            drain(qbuf.at[pl.ds(0, 3)], qr_sem.at[quad])

        @pl.when(j > 0)
        def _():
            drain(qbuf.at[pl.ds(0, 4)], qr_sem.at[quad])

        top, total, numer = attend(quad, 0, me)
        part_n[quad] = numer
        part_m[quad] = jnp.broadcast_to(top, (128, 128))
        part_l[quad] = jnp.broadcast_to(total, (128, 128))
        return carry

    def second_pass(j, carry):
        quad = lax.rem(my_quad + j, 4)
        top, total, numer = attend(quad, 1, partner)
        top_1 = part_m[quad]
        best = jnp.maximum(top_1, top)
        left = jnp.exp2((top_1 - best) * (SCALE * LOG2E))
        right = jnp.exp2((top - best) * (SCALE * LOG2E))
        total = part_l[quad] * left + total * right
        some = total > 0.0
        safe = jnp.where(some, total, 1.0)
        ctx = (part_n[quad] * left + numer * right) / safe
        lse = jnp.where(some, best * (SCALE * LOG2E) + jnp.log2(safe), LOW)
        csend[pl.ds(quad * 4, 4)] = ctx.astype(BF16).reshape(4, ROWS, HD)
        lsend[quad] = lse.T[0:1, :]

        def send_part(t, carry):
            p = quad * 4 + t

            @pl.when(p != z)
            def _():
                to = {"seq": line + p}
                remote(csend.at[p], crecv.at[z], cs_sem, cr_sem, to).start()
                remote(lsend.at[quad], lrecv.at[z], ls_sem, lr_sem, to).start()

            return carry

        lax.fori_loop(0, 4, send_part, 0)
        return carry

    lax.fori_loop(0, 2, first_pass, 0)
    ring_step(0, 2)
    lax.fori_loop(2, 4, first_pass, 0)
    ring_step(0, 3)
    drain(kvt.at[1], xr_sem)
    lax.fori_loop(0, 2, second_pass, 0)
    ring_step(0, 4)
    lax.fori_loop(2, 4, second_pass, 0)
    ring_step(0, 5)
    ring_start(1)
    crecv[z] = csend[z]
    lrecv[z] = lsend[my_quad]
    drain(qbuf.at[pl.ds(0, 15)], qs_sem)
    drain(kvt.at[0], xs_sem)
    ring_step(0, 6)
    ring_step(0, 7)
    drain(crecv.at[pl.ds(0, 15)], cr_sem)
    drain(lrecv.at[pl.ds(0, 15)], lr_sem)

    lmat[...] = jnp.zeros((128, 128), F32)
    for s in range(NZ):
        lmat[s : s + 1, :] = lrecv[s]
    logs = lmat[0:NZ, :]
    share = jnp.exp2(logs - jnp.max(logs, axis=0, keepdims=True))
    lmat[0:NZ, :] = share / jnp.sum(share, axis=0, keepdims=True)
    ltr[...] = lmat[...].T
    mine = ltr[pl.ds(pl.multiple_of(lax.rem(z, 4) * ROWS, ROWS), ROWS), :]
    context = jnp.zeros((ROWS, HD), F32)
    for s in range(NZ):
        context += mine[:, s : s + 1] * crecv[s].astype(F32)

    def scatter_start(n, term):
        for f in range(NLAT):
            rsend[n, f] = term[:, f * HD : (f + 1) * HD].astype(BF16)

        def send(i, carry):
            p = in_lat(i)
            remote(rsend.at[n, p], rrecv.at[n, i], rs_sem.at[n], rr_sem.at[n], {"lat": p}).start()
            return carry

        lax.fori_loop(1, NLAT, send, 0)

    def scatter_finish(n):
        drain(rrecv.at[n, pl.ds(1, NLAT - 1)], rr_sem.at[n])
        acc = rsend[n, lme].astype(F32)
        for i in range(1, NLAT):
            acc += rrecv[n, i].astype(F32)
        return acc

    def gather_start(n, h):
        hsend[n] = h.astype(BF16)
        gath[n, lme] = h.astype(BF16)

        def send(i, carry):
            to = {"lat": in_lat(i)}
            remote(hsend.at[n], gath.at[n, lme], gs_sem.at[n], gr_sem.at[n], to).start()
            return carry

        lax.fori_loop(1, NLAT, send, 0)

    def gather_finish(n):
        drain(gath.at[n, pl.ds(0, NLAT - 1)], gr_sem.at[n])
        rows = jnp.concatenate([gath[n, f] for f in range(NLAT)], axis=1)
        wide = rows.astype(F32)
        gain = lax.rsqrt(jnp.mean(wide * wide, axis=-1, keepdims=True) + 1e-06)
        return rows, gain

    my_cols = pl.ds(pl.multiple_of(lme * HD, HD), HD)
    scatter_start(0, dot_nn(context.astype(BF16), wov[...]))
    ring_step(0, 8)
    move(1, me, partner, wx_sem.at[1]).start()
    h = basev[:, my_cols].astype(F32) + scatter_finish(0)
    gather_start(0, h)
    ring_step(1, 1)
    ring_sent(0)
    ring_finish(0)
    rows, gain = gather_finish(0)
    qkv = (dot_nn(rows, wbuf0[:, :, : 3 * HD].reshape(D, 3 * HD)) * gain).astype(BF16)
    qx[0] = qkv[:, :HD]
    kvbuf[z] = qkv[:, HD:]

    query_out = remote(qx.at[0], qx.at[1], ps_sem.at[0], pr_sem.at[0], {"seq": partner})
    result_out = remote(sx, rx, ps_sem.at[1], pr_sem.at[1], {"seq": partner})

    def kv_send(i, carry):
        remote(kvbuf.at[z], kvbuf.at[z], ks_sem, kr_sem, {"seq": in_line(i)}).start()
        return carry

    lax.fori_loop(1, NZ, kv_send, 0)

    @pl.when(xh == 1)
    def _():
        query_out.start()

    drain(crecv.at[pl.ds(0, 15)], cs_sem)
    drain(lrecv.at[pl.ds(0, 15)], ls_sem)
    ring_step(1, 2)
    ring_step(1, 3)

    @pl.when(xh == 0)
    def _():
        query_out.wait_recv()

    drain(kvbuf.at[pl.ds(0, 15)], kr_sem)
    line_rows = NZ * ROWS
    raw = dot_nt(qx[...].reshape(2 * ROWS, HD), kvbuf[:, :, :HD].reshape(line_rows, HD)) * SCALE
    capped = 30.0 * jnp.tanh(raw / 30.0)
    key_row = lax.broadcasted_iota(jnp.int32, (2 * ROWS, line_rows), 1)
    row = lax.broadcasted_iota(jnp.int32, (2 * ROWS, line_rows), 0)
    seen = (key_row <= z * ROWS + row) | (row >= ROWS)
    expo = jnp.where(seen, jnp.exp(capped), 0.0)
    self_total = jnp.sum(expo, axis=1, keepdims=True)
    self_numer = dot_nn(expo.astype(BF16), kvbuf[:, :, HD:].reshape(line_rows, HD))

    @pl.when(xh == 0)
    def _():
        sx[0:ROWS, :] = self_numer[ROWS:, :]
        sx[ROWS:, :] = jnp.broadcast_to(self_total[ROWS:, :], (ROWS, HD))
        result_out.start()

    ring_step(1, 4)

    @pl.when(xh == 1)
    def _():
        result_out.wait_recv()

    self_ctx = (self_numer[0:ROWS, :] + rx[0:ROWS, :]) / (self_total[0:ROWS, :] + rx[ROWS:, :])

    scatter_start(1, dot_nt(self_ctx.astype(BF16), wbuf0[:, :, 3 * HD :].reshape(D, HD)))
    ring_step(1, 5)
    h = h + scatter_finish(1)
    gather_start(1, h)
    ring_step(1, 6)
    ring_step(1, 7)
    ring_step(1, 8)
    ring_finish(1)
    rows, gain = gather_finish(1)
    hidden = jax.nn.gelu(dot_nn(rows, wbuf1[:, 0].reshape(D, HID)) * gain).astype(BF16)
    part[...] = dot_nt(hidden, wbuf1[:, 1].reshape(D, HID))
    part[:, my_cols] += h
    for f in range(NLAT):
        fsend[f] = part[2 * f : 2 * f + 2, :]

    def last_send(i, carry):
        p = in_lat(i)
        remote(fsend.at[p], frecv.at[i], fs_sem, fr_sem, {"lat": p}).start()
        return carry

    lax.fori_loop(1, NLAT, last_send, 0)
    ring_sent(1)
    for n in range(2):
        drain(rrecv.at[n, pl.ds(1, NLAT - 1)], rs_sem.at[n])
        drain(gath.at[n, pl.ds(0, NLAT - 1)], gs_sem.at[n])
    drain(kvbuf.at[pl.ds(0, 15)], ks_sem)

    @pl.when(xh == 1)
    def _():
        query_out.wait_send()

    @pl.when(xh == 0)
    def _():
        result_out.wait_send()

    drain(frecv.at[pl.ds(1, NLAT - 1)], fr_sem)
    acc = fsend[lme]
    for i in range(1, NLAT):
        acc += frecv[i]
    out_ref[...] = acc.astype(BF16)
    drain(frecv.at[pl.ds(1, NLAT - 1)], fs_sem)


def local(
    inputs,
    cross_kv,
    cross_out_w,
    latent_query,
    latent_base,
    latent_pos,
    attn_qkv,
    attn_out,
    mlp_up,
    mlp_down,
):
    dma = pltpu.SemaphoreType.DMA
    vmem = pl.BlockSpec(memory_space=pltpu.VMEM)
    hbm = pl.BlockSpec(memory_space=pltpu.HBM)
    return pl.pallas_call(
        kernel,
        out_shape=jax.ShapeDtypeStruct((ROWS // NLAT, D), BF16),
        in_specs=[hbm] * 10,
        out_specs=vmem,
        scratch_shapes=[
            pltpu.VMEM((TOK, D), BF16),
            pltpu.VMEM((D, 2 * HD), BF16),
            pltpu.VMEM((HD, D), BF16),
            pltpu.VMEM((ROWS, D), BF16),
            pltpu.VMEM((8, 128), jnp.int32),
            pltpu.VMEM((2, TOK, 2 * HD), BF16),
            pltpu.VMEM((NZ, ROWS, HD), BF16),
            pltpu.VMEM((NSEQ, CHUNK, HID), BF16),
            pltpu.VMEM((NSEQ, 2, CHUNK, HID), BF16),
            pltpu.VMEM((4, 128, 128), F32),
            pltpu.VMEM((4, 128, 128), F32),
            pltpu.VMEM((4, 128, 128), F32),
            pltpu.VMEM((NZ, ROWS, HD), BF16),
            pltpu.VMEM((NZ, ROWS, HD), BF16),
            pltpu.VMEM((4, 1, 128), F32),
            pltpu.VMEM((NZ, 1, 128), F32),
            pltpu.VMEM((128, 128), F32),
            pltpu.VMEM((128, 128), F32),
            pltpu.VMEM((2, NLAT, ROWS, HD), BF16),
            pltpu.VMEM((2, NLAT, ROWS, HD), BF16),
            pltpu.VMEM((2, ROWS, HD), BF16),
            pltpu.VMEM((2, NLAT, ROWS, HD), BF16),
            pltpu.VMEM((NZ, ROWS, 2 * HD), BF16),
            pltpu.VMEM((2, ROWS, HD), BF16),
            pltpu.VMEM((2 * ROWS, HD), F32),
            pltpu.VMEM((2 * ROWS, HD), F32),
            pltpu.VMEM((ROWS, D), F32),
            pltpu.VMEM((NLAT, 2, D), F32),
            pltpu.VMEM((NLAT, 2, D), F32),
            dma((12,)),
            dma,
            dma((4,)),
            dma,
            dma,
            dma((2,)),
            dma((2, 9)),
            dma((2, 9)),
            dma((2,)),
            dma,
            dma,
            dma,
            dma,
            dma((2,)),
            dma((2,)),
            dma((2,)),
            dma((2,)),
            dma,
            dma,
            dma((2,)),
            dma((2,)),
            dma,
            dma,
        ],
        compiler_params=pltpu.CompilerParams(
            collective_id=0, has_side_effects=True, vmem_limit_bytes=63 << 20
        ),
    )(
        inputs,
        cross_kv.reshape(D, 2 * HD),
        cross_out_w,
        latent_query,
        latent_base,
        latent_pos.reshape(8, 128),
        jnp.swapaxes(attn_qkv[0], 0, 1),
        attn_out[0],
        mlp_up[0],
        mlp_down[0],
    )


def solution(mesh):
    return jax.shard_map(
        local,
        mesh=mesh,
        in_specs=(
            P("seq", None),
            P(None, None, "lat"),
            P("lat", None),
            P("seq", "lat"),
            P("seq", None),
            P(),
            P(None, "seq", None, "lat"),
            P(None, "seq", "lat"),
            P(None, "seq", "lat"),
            P(None, "seq", "lat"),
        ),
        out_specs=P(("seq", "lat"), None),
        check_vma=False,
    )
```

```python
import math

import jax
import jax.numpy as jnp
from jax import lax
from jax.experimental import pallas as pl
from jax.experimental.pallas import tpu as pltpu
from jax.sharding import PartitionSpec as P

HD = 128
NSEQ = 32
NZ = 16
NLAT = 16
ROWS = 32
LATENTS = 1024
TOK = 768
D = 2048
HID = 512
CHUNK = 64
MESH = pl.DeviceIdType.MESH
F32 = jnp.float32
BF16 = jnp.bfloat16
LOG2E = 1.4426950408889634
SCALE = 1.0 / math.sqrt(HD)
LOW = -1e30


def dot_nt(a, b):
    return lax.dot_general(a, b, (((1,), (1,)), ((), ())), preferred_element_type=F32)


def dot_nn(a, b):
    return jnp.dot(a, b, preferred_element_type=F32)


def kernel(
    x_hbm,
    ckv_hbm,
    wo_hbm,
    q_hbm,
    base_hbm,
    pos_hbm,
    qkv_hbm,
    ow_hbm,
    up_hbm,
    down_hbm,
    out_ref,
    xv,
    ckvv,
    wov,
    basev,
    posv,
    kvt,
    qbuf,
    wbuf0,
    wbuf1,
    part_n,
    part_m,
    part_l,
    csend,
    crecv,
    lsend,
    lrecv,
    lmat,
    ltr,
    rsend,
    rrecv,
    hsend,
    gath,
    kvbuf,
    qx,
    sx,
    rx,
    wide_in,
    up_out,
    up_in,
    part,
    fsend,
    frecv,
    load_sem,
    qs_sem,
    qr_sem,
    xs_sem,
    xr_sem,
    ws_sem,
    wf_sem,
    wb_sem,
    wx_sem,
    cs_sem,
    cr_sem,
    ls_sem,
    lr_sem,
    rs_sem,
    rr_sem,
    gs_sem,
    gr_sem,
    ks_sem,
    kr_sem,
    ps_sem,
    pr_sem,
    fs_sem,
    fr_sem,
):
    me = lax.axis_index("seq")
    lme = lax.axis_index("lat")
    xh = me // NZ
    z = lax.rem(me, NZ)
    line = xh * NZ
    partner = lax.rem(me + NZ, NSEQ)
    my_quad = z // 4
    z_up = line + lax.rem(z + 1, NZ)
    z_down = line + lax.rem(z + NZ - 1, NZ)

    loads = [
        pltpu.make_async_copy(src, dst, load_sem.at[n])
        for n, (src, dst) in enumerate(
            (
                (q_hbm, qbuf.at[z]),
                (qkv_hbm.at[0], wbuf0.at[me, :, pl.ds(0, HD)]),
                (qkv_hbm.at[1], wbuf0.at[me, :, pl.ds(HD, HD)]),
                (qkv_hbm.at[2], wbuf0.at[me, :, pl.ds(2 * HD, HD)]),
                (ow_hbm, wbuf0.at[me, :, pl.ds(3 * HD, HD)]),
                (ckv_hbm, ckvv),
                (x_hbm, xv),
                (up_hbm, wbuf1.at[z, 0]),
                (down_hbm, wbuf1.at[z, 1]),
                (pos_hbm, posv),
                (wo_hbm, wov),
                (base_hbm, basev),
            )
        )
    ]
    for load in loads:
        load.start()

    barrier = pltpu.get_barrier_semaphore()

    def greet(device_id):
        pl.semaphore_signal(barrier, inc=1, device_id=device_id, device_id_type=MESH)

    def in_line(i):
        return line + lax.rem(z + i, NZ)

    def in_lat(i):
        return lax.rem(lme + i, NLAT)

    def greet_all(i, carry):
        greet({"seq": in_line(i)})
        greet({"lat": in_lat(i)})
        greet({"seq": partner, "lat": in_lat(i)})
        return carry

    lax.fori_loop(1, NZ, greet_all, 0)
    qx[1] = jnp.zeros((ROWS, HD), BF16)
    rx[...] = jnp.zeros_like(rx)
    greet({"seq": partner})
    for load in loads[:5]:
        load.wait()
    pl.semaphore_wait(barrier, NZ - 1 + 1 + 2 * (NLAT - 1))

    def drain(ref, sem):
        pltpu.make_async_copy(ref, ref, sem).wait()

    def remote(src, dst, send_sem, recv_sem, device_id):
        return pltpu.make_async_remote_copy(
            src_ref=src,
            dst_ref=dst,
            send_sem=send_sem,
            recv_sem=recv_sem,
            device_id=device_id,
            device_id_type=MESH,
        )

    def send_query(i, carry):
        remote(qbuf.at[z], qbuf.at[z], qs_sem, qr_sem.at[my_quad], {"seq": in_line(i)}).start()
        return carry

    lax.fori_loop(1, NZ, send_query, 0)

    def chunk(r, place):
        return wbuf0.at[line + place] if r == 0 else wbuf1.at[place]

    def move(r, place, to, recv_sem):
        ref = chunk(r, place)
        return remote(ref, ref, ws_sem.at[r], recv_sem, {"seq": to})

    def ring_start(r):
        move(r, z, z_up, wf_sem.at[r, 1]).start()
        move(r, z, z_down, wb_sem.at[r, 1]).start()

    def ring_step(r, k):
        low = lax.rem(z + NZ - k, NZ)
        high = lax.rem(z + k, NZ)
        move(r, low, z_up, wf_sem.at[r, k]).wait_recv()
        if k < 8:
            move(r, low, z_up, wf_sem.at[r, k + 1]).start()
            move(r, high, z_down, wb_sem.at[r, k]).wait_recv()
            if k < 7:
                move(r, high, z_down, wb_sem.at[r, k + 1]).start()

    def cross(k):
        move(0, lax.rem(z + NZ - k, NZ), partner, wx_sem).start()
        if 0 < k < 8:
            move(0, lax.rem(z + k, NZ), partner, wx_sem).start()

    ring_start(0)

    loads[5].wait()
    loads[6].wait()
    half_rows = TOK // 2
    for half in range(2):
        rows = pl.ds(half * half_rows, half_rows)
        kvt[0, rows, :] = dot_nn(xv[rows, :], ckvv[...]).astype(BF16)
        remote(kvt.at[0, rows], kvt.at[1, rows], xs_sem, xr_sem, {"seq": partner}).start()
    for load in loads[7:]:
        load.wait()
    ring_step(0, 1)

    def attend(quad, slot, owner):
        q = qbuf[pl.ds(quad * 4, 4)].reshape(4 * ROWS, HD)
        scores = dot_nt(q, kvt[slot, :, :HD])
        row = posv[pl.ds(xh * 4 + quad, 1), :].astype(F32)
        pos = jnp.broadcast_to(row, (128, 128)).T[:, 0:1]
        key = lax.broadcasted_iota(jnp.int32, (1, TOK), 1) + owner * TOK
        allowed = key.astype(F32) <= pos
        top = jnp.max(jnp.where(allowed, scores, LOW), axis=1, keepdims=True)
        weights = jnp.where(allowed, jnp.exp2((scores - top) * (SCALE * LOG2E)), 0.0)
        total = jnp.sum(weights, axis=1, keepdims=True)
        numer = dot_nn(weights.astype(BF16), kvt[slot, :, HD:])
        return top, total, numer

    def first_pass(j, carry):
        quad = lax.rem(my_quad + j, 4)

        @pl.when(j == 0)
        def _():
            drain(qbuf.at[pl.ds(0, 3)], qr_sem.at[quad])

        @pl.when(j > 0)
        def _():
            drain(qbuf.at[pl.ds(0, 4)], qr_sem.at[quad])

        top, total, numer = attend(quad, 0, me)
        part_n[quad] = numer
        part_m[quad] = jnp.broadcast_to(top, (128, 128))
        part_l[quad] = jnp.broadcast_to(total, (128, 128))
        return carry

    def second_pass(j, carry):
        quad = lax.rem(my_quad + j, 4)
        top, total, numer = attend(quad, 1, partner)
        top_1 = part_m[quad]
        best = jnp.maximum(top_1, top)
        left = jnp.exp2((top_1 - best) * (SCALE * LOG2E))
        right = jnp.exp2((top - best) * (SCALE * LOG2E))
        total = part_l[quad] * left + total * right
        some = total > 0.0
        safe = jnp.where(some, total, 1.0)
        ctx = (part_n[quad] * left + numer * right) / safe
        lse = jnp.where(some, best * (SCALE * LOG2E) + jnp.log2(safe), LOW)
        csend[pl.ds(quad * 4, 4)] = ctx.astype(BF16).reshape(4, ROWS, HD)
        lsend[quad] = lse.T[0:1, :]

        def send_part(t, carry):
            p = quad * 4 + t

            @pl.when(p != z)
            def _():
                to = {"seq": line + p}
                remote(csend.at[p], crecv.at[z], cs_sem, cr_sem, to).start()
                remote(lsend.at[quad], lrecv.at[z], ls_sem, lr_sem, to).start()

            return carry

        lax.fori_loop(0, 4, send_part, 0)
        return carry

    lax.fori_loop(0, 2, first_pass, 0)
    ring_step(0, 2)
    lax.fori_loop(2, 4, first_pass, 0)
    ring_step(0, 3)
    drain(kvt.at[1], xr_sem)
    for k in range(3):
        cross(k)
    lax.fori_loop(0, 2, second_pass, 0)
    ring_step(0, 4)
    cross(3)
    lax.fori_loop(2, 4, second_pass, 0)
    ring_step(0, 5)
    cross(4)
    ring_start(1)
    crecv[z] = csend[z]
    lrecv[z] = lsend[my_quad]
    drain(qbuf.at[pl.ds(0, 15)], qs_sem)
    drain(kvt.at[0], xs_sem)
    ring_step(0, 6)
    cross(5)
    ring_step(0, 7)
    cross(6)
    ring_step(0, 8)
    cross(7)
    cross(8)
    ring_step(1, 1)
    drain(crecv.at[pl.ds(0, 15)], cr_sem)
    drain(lrecv.at[pl.ds(0, 15)], lr_sem)

    lmat[...] = jnp.zeros((128, 128), F32)
    for s in range(NZ):
        lmat[s : s + 1, :] = lrecv[s]
    logs = lmat[0:NZ, :]
    share = jnp.exp2(logs - jnp.max(logs, axis=0, keepdims=True))
    lmat[0:NZ, :] = share / jnp.sum(share, axis=0, keepdims=True)
    ltr[...] = lmat[...].T
    mine = ltr[pl.ds(pl.multiple_of(lax.rem(z, 4) * ROWS, ROWS), ROWS), :]
    context = jnp.zeros((ROWS, HD), F32)
    for s in range(NZ):
        context += mine[:, s : s + 1] * crecv[s].astype(F32)

    def scatter_start(n, term):
        for f in range(NLAT):
            rsend[n, f] = term[:, f * HD : (f + 1) * HD].astype(BF16)

        def send(i, carry):
            p = in_lat(i)
            remote(rsend.at[n, p], rrecv.at[n, i], rs_sem.at[n], rr_sem.at[n], {"lat": p}).start()
            return carry

        lax.fori_loop(1, NLAT, send, 0)

    def scatter_finish(n):
        drain(rrecv.at[n, pl.ds(1, NLAT - 1)], rr_sem.at[n])
        acc = rsend[n, lme].astype(F32)
        for i in range(1, NLAT):
            acc += rrecv[n, i].astype(F32)
        return acc

    def gather_start(h):
        hsend[0] = h.astype(BF16)
        gath[lme] = h.astype(BF16)

        def send(i, carry):
            to = {"lat": in_lat(i)}
            remote(hsend.at[0], gath.at[lme], gs_sem.at[0], gr_sem.at[0], to).start()
            return carry

        lax.fori_loop(1, NLAT, send, 0)

    def gather_finish():
        drain(gath.at[pl.ds(0, NLAT - 1)], gr_sem.at[0])
        return jnp.concatenate([gath[f] for f in range(NLAT)], axis=1)

    my_cols = pl.ds(pl.multiple_of(lme * HD, HD), HD)
    scatter_start(0, dot_nn(context.astype(BF16), wov[...]))
    ring_step(1, 2)
    h = basev[:, my_cols].astype(F32) + scatter_finish(0)
    gather_start(h)
    ring_step(1, 3)
    drain(wbuf0.at[pl.ds(0, 31)], ws_sem.at[0])
    drain(wbuf0.at[pl.ds((1 - xh) * NZ, NZ)], wx_sem)
    rows = gather_finish()
    wide = rows.astype(F32)
    gain = lax.rsqrt(jnp.mean(wide * wide, axis=-1, keepdims=True) + 1e-06)
    qkv = (dot_nn(rows, wbuf0[:, :, : 3 * HD].reshape(D, 3 * HD)) * gain).astype(BF16)
    qx[0] = qkv[:, :HD]
    kvbuf[z] = qkv[:, HD:]

    query_out = remote(qx.at[0], qx.at[1], ps_sem.at[0], pr_sem.at[0], {"seq": partner})
    result_out = remote(sx, rx, ps_sem.at[1], pr_sem.at[1], {"seq": partner})

    def kv_move(place, i, n):
        ref = kvbuf.at[lax.rem(place, NZ)]
        return remote(ref, ref, ks_sem, kr_sem.at[n], {"seq": in_line(i)})

    for i in (4, 12, 1, 15, 2, 14, 3, 13):
        kv_move(z, i, {4: 1, 12: 2}.get(i, 0)).start()

    @pl.when(xh == 1)
    def _():
        query_out.start()

    drain(crecv.at[pl.ds(0, 15)], cs_sem)
    drain(lrecv.at[pl.ds(0, 15)], ls_sem)
    kv_move(z + 12, 4, 1).wait_recv()
    for i in range(1, 5):
        kv_move(z + 12, i, 0).start()
    kv_move(z + 4, 12, 2).wait_recv()
    for i in range(13, 16):
        kv_move(z + 4, i, 0).start()
    ring_step(1, 4)
    ring_step(1, 5)

    @pl.when(xh == 0)
    def _():
        query_out.wait_recv()

    drain(kvbuf.at[pl.ds(0, 13)], kr_sem.at[0])
    line_rows = NZ * ROWS
    raw = dot_nt(qx[...].reshape(2 * ROWS, HD), kvbuf[:, :, :HD].reshape(line_rows, HD)) * SCALE
    capped = 30.0 * jnp.tanh(raw / 30.0)
    key_row = lax.broadcasted_iota(jnp.int32, (2 * ROWS, line_rows), 1)
    row = lax.broadcasted_iota(jnp.int32, (2 * ROWS, line_rows), 0)
    seen = (key_row <= z * ROWS + row) | (row >= ROWS)
    expo = jnp.where(seen, jnp.exp(capped), 0.0)
    self_total = jnp.sum(expo, axis=1, keepdims=True)
    self_numer = dot_nn(expo.astype(BF16), kvbuf[:, :, HD:].reshape(line_rows, HD))

    @pl.when(xh == 0)
    def _():
        sx[0:ROWS, :] = self_numer[ROWS:, :]
        sx[ROWS:, :] = jnp.broadcast_to(self_total[ROWS:, :], (ROWS, HD))
        result_out.start()

    ring_step(1, 6)

    @pl.when(xh == 1)
    def _():
        result_out.wait_recv()

    self_ctx = (self_numer[0:ROWS, :] + rx[0:ROWS, :]) / (self_total[0:ROWS, :] + rx[ROWS:, :])

    scatter_start(1, dot_nt(self_ctx.astype(BF16), wbuf0[:, :, 3 * HD :].reshape(D, HD)))
    ring_step(1, 7)
    h = h + scatter_finish(1)

    home = lme // 8
    col = lax.rem(lme, 8)
    at_home = xh == home
    hsend[1] = h.astype(BF16)

    def wide_send(i, carry):
        @pl.when(jnp.logical_or(i != lme, xh != home))
        def _():
            to = {"seq": home * NZ + z, "lat": i}
            remote(hsend.at[1], wide_in.at[xh, col], gs_sem.at[1], gr_sem.at[1], to).start()

        return carry

    def wide_wait(sem):
        @pl.when(at_home)
        def _():
            drain(gath.at[pl.ds(0, 15)], sem)

        @pl.when(jnp.logical_not(at_home))
        def _():
            drain(gath.at[pl.ds(0, 16)], sem)

    lax.fori_loop(0, NLAT, wide_send, 0)

    @pl.when(at_home)
    def _():
        wide_in[xh, col] = hsend[1]

    ring_step(1, 8)
    wide_wait(gr_sem.at[1])
    rows = jnp.concatenate([wide_in[:, f].reshape(2 * ROWS, HD) for f in range(8)], axis=1)
    wide = rows.astype(F32)
    square = jnp.sum(wide * wide, axis=-1, keepdims=True)
    up = dot_nn(rows, wbuf1[:, 0].reshape(D // 2, HID))
    up_out[:, 0:HID] = up.astype(BF16)
    high = jnp.broadcast_to(square, (2 * ROWS, HD)).astype(BF16).astype(F32)
    lane = lax.broadcasted_iota(jnp.int32, (2 * ROWS, HD), 1)
    up_out[:, HID:] = jnp.where(lane < HD // 2, high, square - high).astype(BF16)
    half_out = remote(up_out, up_in, ps_sem.at[2], pr_sem.at[2], {"seq": partner})
    half_out.start()
    drain(wbuf1.at[pl.ds(0, 15)], ws_sem.at[1])
    for n in range(2):
        drain(rrecv.at[n, pl.ds(1, NLAT - 1)], rs_sem.at[n])
    drain(gath.at[pl.ds(0, NLAT - 1)], gs_sem.at[0])
    wide_wait(gs_sem.at[1])
    drain(kvbuf.at[pl.ds(0, 15)], ks_sem)
    half_out.wait_recv()
    other = up_in[:, HID:].astype(F32)
    square = square + other[:, 0:1] + other[:, HD // 2 : HD // 2 + 1]
    gain = lax.rsqrt(square * (1.0 / D) + 1e-06)
    hidden = jax.nn.gelu((up + up_in[:, 0:HID].astype(F32)) * gain).astype(BF16)
    part[...] = dot_nt(hidden, wbuf1[:, 1].reshape(D // 2, HID))

    @pl.when(at_home)
    def _():
        cols = pl.ds(pl.multiple_of(col * HD, HD), HD)
        part[:, cols] += wide_in[:, col].reshape(2 * ROWS, HD).astype(F32)

    for f in range(2 * NLAT):
        fsend[f] = part[2 * f : 2 * f + 2, :]
    mine = xh * NLAT + lme

    def last_send(i, carry):
        p = lax.rem(mine + i, 2 * NLAT)
        to = {"seq": (p // NLAT) * NZ + z, "lat": lax.rem(p, NLAT)}
        remote(fsend.at[p], frecv.at[mine], fs_sem, fr_sem, to).start()
        return carry

    lax.fori_loop(1, 2 * NLAT, last_send, 0)
    frecv[mine] = fsend[mine]
    half_out.wait_send()

    @pl.when(xh == 1)
    def _():
        query_out.wait_send()

    @pl.when(xh == 0)
    def _():
        result_out.wait_send()

    drain(frecv.at[pl.ds(0, 31)], fr_sem)
    for half in range(2):
        acc = frecv[half * NLAT]
        for i in range(1, NLAT):
            acc += frecv[half * NLAT + i]
        out_ref[:, half * (D // 2) : (half + 1) * (D // 2)] = acc.astype(BF16)
    drain(frecv.at[pl.ds(0, 31)], fs_sem)


def local(
    inputs,
    cross_kv,
    cross_out_w,
    latent_query,
    latent_base,
    latent_pos,
    attn_qkv,
    attn_out,
    mlp_up,
    mlp_down,
):
    dma = pltpu.SemaphoreType.DMA
    vmem = pl.BlockSpec(memory_space=pltpu.VMEM)
    hbm = pl.BlockSpec(memory_space=pltpu.HBM)
    return pl.pallas_call(
        kernel,
        out_shape=jax.ShapeDtypeStruct((ROWS // NLAT, D), BF16),
        in_specs=[hbm] * 10,
        out_specs=vmem,
        scratch_shapes=[
            pltpu.VMEM((TOK, D), BF16),
            pltpu.VMEM((D, 2 * HD), BF16),
            pltpu.VMEM((HD, D), BF16),
            pltpu.VMEM((ROWS, D), BF16),
            pltpu.VMEM((8, 128), jnp.int32),
            pltpu.VMEM((2, TOK, 2 * HD), BF16),
            pltpu.VMEM((NZ, ROWS, HD), BF16),
            pltpu.VMEM((NSEQ, CHUNK, HID), BF16),
            pltpu.VMEM((NZ, 2, CHUNK, HID), BF16),
            pltpu.VMEM((4, 128, 128), F32),
            pltpu.VMEM((4, 128, 128), F32),
            pltpu.VMEM((4, 128, 128), F32),
            pltpu.VMEM((NZ, ROWS, HD), BF16),
            pltpu.VMEM((NZ, ROWS, HD), BF16),
            pltpu.VMEM((4, 1, 128), F32),
            pltpu.VMEM((NZ, 1, 128), F32),
            pltpu.VMEM((128, 128), F32),
            pltpu.VMEM((128, 128), F32),
            pltpu.VMEM((2, NLAT, ROWS, HD), BF16),
            pltpu.VMEM((2, NLAT, ROWS, HD), BF16),
            pltpu.VMEM((2, ROWS, HD), BF16),
            pltpu.VMEM((NLAT, ROWS, HD), BF16),
            pltpu.VMEM((NZ, ROWS, 2 * HD), BF16),
            pltpu.VMEM((2, ROWS, HD), BF16),
            pltpu.VMEM((2 * ROWS, HD), F32),
            pltpu.VMEM((2 * ROWS, HD), F32),
            pltpu.VMEM((2, 8, ROWS, HD), BF16),
            pltpu.VMEM((2 * ROWS, HID + HD), BF16),
            pltpu.VMEM((2 * ROWS, HID + HD), BF16),
            pltpu.VMEM((2 * ROWS, D // 2), F32),
            pltpu.VMEM((2 * NLAT, 2, D // 2), F32),
            pltpu.VMEM((2 * NLAT, 2, D // 2), F32),
            dma((12,)),
            dma,
            dma((4,)),
            dma,
            dma,
            dma((2,)),
            dma((2, 9)),
            dma((2, 9)),
            dma,
            dma,
            dma,
            dma,
            dma,
            dma((2,)),
            dma((2,)),
            dma((2,)),
            dma((2,)),
            dma,
            dma((3,)),
            dma((3,)),
            dma((3,)),
            dma,
            dma,
        ],
        compiler_params=pltpu.CompilerParams(
            collective_id=0, has_side_effects=True, vmem_limit_bytes=63 << 20
        ),
    )(
        inputs,
        cross_kv.reshape(D, 2 * HD),
        cross_out_w,
        latent_query,
        latent_base,
        latent_pos.reshape(8, 128),
        jnp.swapaxes(attn_qkv[0], 0, 1),
        attn_out[0],
        mlp_up[0],
        mlp_down[0],
    )


def solution(mesh):
    return jax.shard_map(
        local,
        mesh=mesh,
        in_specs=(
            P("seq", None),
            P(None, None, "lat"),
            P("lat", None),
            P("seq", "lat"),
            P("seq", None),
            P(),
            P(None, "seq", None, "lat"),
            P(None, "seq", "lat"),
            P(None, "seq", "lat"),
            P(None, "seq", "lat"),
        ),
        out_specs=P(("seq", "lat"), None),
        check_vma=False,
    )
```

```python
import math

import jax
import jax.numpy as jnp
from jax import lax
from jax.experimental import pallas as pl
from jax.experimental.pallas import tpu as pltpu
from jax.sharding import PartitionSpec as P

HD = 128
NSEQ = 32
NZ = 16
NLAT = 16
ROWS = 32
LATENTS = 1024
TOK = 768
D = 2048
HID = 512
CHUNK = 64
MESH = pl.DeviceIdType.MESH
F32 = jnp.float32
BF16 = jnp.bfloat16
LOG2E = 1.4426950408889634
SCALE = 1.0 / math.sqrt(HD)
LOW = -1e30


def dot_nt(a, b):
    return lax.dot_general(a, b, (((1,), (1,)), ((), ())), preferred_element_type=F32)


def dot_nn(a, b):
    return jnp.dot(a, b, preferred_element_type=F32)


def kernel(
    x_hbm,
    ckv_hbm,
    wo_hbm,
    q_hbm,
    base_hbm,
    pos_hbm,
    qkv_hbm,
    ow_hbm,
    up_hbm,
    down_hbm,
    out_ref,
    xv,
    ckvv,
    wov,
    basev,
    posv,
    kvt,
    qbuf,
    wbuf0,
    wbuf1,
    part_n,
    part_m,
    part_l,
    csend,
    crecv,
    lsend,
    lrecv,
    lmat,
    ltr,
    rsend,
    rrecv,
    hsend,
    gath,
    kvbuf,
    qx,
    sx,
    rx,
    wide_in,
    up_out,
    up_in,
    part,
    ftile,
    fsend,
    frecv,
    load_sem,
    qs_sem,
    qr_sem,
    xs_sem,
    xr_sem,
    ws_sem,
    wf_sem,
    wb_sem,
    wx_sem,
    cs_sem,
    cr_sem,
    ls_sem,
    lr_sem,
    rs_sem,
    rr_sem,
    gs_sem,
    gr_sem,
    ks_sem,
    kr_sem,
    ps_sem,
    pr_sem,
    fs_sem,
    fr_sem,
):
    me = lax.axis_index("seq")
    lme = lax.axis_index("lat")
    xh = me // NZ
    z = lax.rem(me, NZ)
    line = xh * NZ
    partner = lax.rem(me + NZ, NSEQ)
    my_quad = z // 4
    z_up = line + lax.rem(z + 1, NZ)
    z_down = line + lax.rem(z + NZ - 1, NZ)

    loads = [
        pltpu.make_async_copy(src, dst, load_sem.at[n])
        for n, (src, dst) in enumerate(
            (
                (ckv_hbm, ckvv),
                (x_hbm, xv),
                (q_hbm, qbuf.at[z]),
                (qkv_hbm.at[0], wbuf0.at[me, :, pl.ds(0, HD)]),
                (qkv_hbm.at[1], wbuf0.at[me, :, pl.ds(HD, HD)]),
                (qkv_hbm.at[2], wbuf0.at[me, :, pl.ds(2 * HD, HD)]),
                (ow_hbm, wbuf0.at[me, :, pl.ds(3 * HD, HD)]),
                (up_hbm, wbuf1.at[z, 0]),
                (down_hbm, wbuf1.at[z, 1]),
                (pos_hbm, posv),
                (wo_hbm, wov),
                (base_hbm, basev),
            )
        )
    ]
    for load in loads:
        load.start()

    barrier = pltpu.get_barrier_semaphore()

    def greet(device_id):
        pl.semaphore_signal(barrier, inc=1, device_id=device_id, device_id_type=MESH)

    def in_line(i):
        return line + lax.rem(z + i, NZ)

    def in_lat(i):
        return lax.rem(lme + i, NLAT)

    def greet_all(i, carry):
        greet({"seq": in_line(i)})
        greet({"lat": in_lat(i)})
        greet({"seq": partner, "lat": in_lat(i)})
        return carry

    lax.fori_loop(1, NZ, greet_all, 0)
    qx[1] = jnp.zeros((ROWS, HD), BF16)
    rx[...] = jnp.zeros_like(rx)
    greet({"seq": partner})
    loads[2].wait()
    pl.semaphore_wait(barrier, NZ - 1 + 1 + 2 * (NLAT - 1))

    def drain(ref, sem):
        pltpu.make_async_copy(ref, ref, sem).wait()

    def remote(src, dst, send_sem, recv_sem, device_id):
        return pltpu.make_async_remote_copy(
            src_ref=src,
            dst_ref=dst,
            send_sem=send_sem,
            recv_sem=recv_sem,
            device_id=device_id,
            device_id_type=MESH,
        )

    def send_query(n, carry):
        i = 8 + (1 - 2 * lax.rem(n, 2)) * (n // 2)
        remote(qbuf.at[z], qbuf.at[z], qs_sem, qr_sem.at[my_quad], {"seq": in_line(i)}).start()
        return carry

    lax.fori_loop(1, NZ, send_query, 0)

    def chunk(r, place):
        return wbuf0.at[line + place] if r == 0 else wbuf1.at[place]

    def move(r, place, to, recv_sem):
        ref = chunk(r, place)
        return remote(ref, ref, ws_sem.at[r], recv_sem, {"seq": to})

    def ring_start(r):
        move(r, z, z_up, wf_sem.at[r, 1]).start()
        move(r, z, z_down, wb_sem.at[r, 1]).start()

    def ring_step(r, k):
        low = lax.rem(z + NZ - k, NZ)
        high = lax.rem(z + k, NZ)
        move(r, low, z_up, wf_sem.at[r, k]).wait_recv()
        if k < 8:
            move(r, low, z_up, wf_sem.at[r, k + 1]).start()
            move(r, high, z_down, wb_sem.at[r, k]).wait_recv()
            if k < 7:
                move(r, high, z_down, wb_sem.at[r, k + 1]).start()

    def cross(k):
        move(0, lax.rem(z + NZ - k, NZ), partner, wx_sem).start()
        if 0 < k < 8:
            move(0, lax.rem(z + k, NZ), partner, wx_sem).start()

    loads[0].wait()
    loads[1].wait()
    piece = TOK // 4
    for n in range(4):
        rows = pl.ds(n * piece, piece)
        kvt[0, rows, :] = dot_nn(xv[rows, :], ckvv[...]).astype(BF16)
        remote(kvt.at[0, rows], kvt.at[1, rows], xs_sem, xr_sem, {"seq": partner}).start()
        if n == 0:
            for load in loads[3:7]:
                load.wait()
            ring_start(0)
    for load in loads[7:]:
        load.wait()
    ring_step(0, 1)

    def attend(quad, slot, owner):
        q = qbuf[pl.ds(quad * 4, 4)].reshape(4 * ROWS, HD)
        scores = dot_nt(q, kvt[slot, :, :HD])
        row = posv[pl.ds(xh * 4 + quad, 1), :].astype(F32)
        pos = jnp.broadcast_to(row, (128, 128)).T[:, 0:1]
        key = lax.broadcasted_iota(jnp.int32, (1, TOK), 1) + owner * TOK
        allowed = key.astype(F32) <= pos
        top = jnp.max(jnp.where(allowed, scores, LOW), axis=1, keepdims=True)
        weights = jnp.where(allowed, jnp.exp2((scores - top) * (SCALE * LOG2E)), 0.0)
        total = jnp.sum(weights, axis=1, keepdims=True)
        numer = dot_nn(weights.astype(BF16), kvt[slot, :, HD:])
        return top, total, numer

    def first_pass(j, carry):
        quad = lax.rem(my_quad + j, 4)

        @pl.when(j == 0)
        def _():
            drain(qbuf.at[pl.ds(0, 3)], qr_sem.at[quad])

        @pl.when(j > 0)
        def _():
            drain(qbuf.at[pl.ds(0, 4)], qr_sem.at[quad])

        top, total, numer = attend(quad, 0, me)
        part_n[quad] = numer
        part_m[quad] = jnp.broadcast_to(top, (128, 128))
        part_l[quad] = jnp.broadcast_to(total, (128, 128))
        return carry

    def second_pass(j, carry):
        quad = lax.rem(my_quad + 1 + j, 4)
        top, total, numer = attend(quad, 1, partner)
        top_1 = part_m[quad]
        best = jnp.maximum(top_1, top)
        left = jnp.exp2((top_1 - best) * (SCALE * LOG2E))
        right = jnp.exp2((top - best) * (SCALE * LOG2E))
        total = part_l[quad] * left + total * right
        some = total > 0.0
        safe = jnp.where(some, total, 1.0)
        ctx = (part_n[quad] * left + numer * right) / safe
        lse = jnp.where(some, best * (SCALE * LOG2E) + jnp.log2(safe), LOW)
        csend[pl.ds(quad * 4, 4)] = ctx.astype(BF16).reshape(4, ROWS, HD)
        lsend[quad] = lse.T[0:1, :]

        def send_part(t, carry):
            p = quad * 4 + t

            @pl.when(p != z)
            def _():
                to = {"seq": line + p}
                remote(csend.at[p], crecv.at[z], cs_sem, cr_sem, to).start()
                remote(lsend.at[quad], lrecv.at[z], ls_sem, lr_sem, to).start()

            return carry

        lax.fori_loop(0, 4, send_part, 0)
        return carry

    lax.fori_loop(0, 2, first_pass, 0)
    ring_step(0, 2)
    lax.fori_loop(2, 4, first_pass, 0)
    drain(kvt.at[1], xr_sem)
    ring_step(0, 3)
    lax.fori_loop(0, 4, second_pass, 0)
    ring_step(0, 4)
    ring_start(1)
    for k in range(5):
        cross(k)
    crecv[z] = csend[z]
    lrecv[z] = lsend[my_quad]
    drain(qbuf.at[pl.ds(0, 15)], qs_sem)
    drain(kvt.at[0], xs_sem)
    ring_step(0, 5)
    cross(5)
    ring_step(1, 1)
    ring_step(0, 6)
    cross(6)
    drain(crecv.at[pl.ds(0, 15)], cr_sem)
    drain(lrecv.at[pl.ds(0, 15)], lr_sem)

    lmat[...] = jnp.zeros((128, 128), F32)
    for s in range(NZ):
        lmat[s : s + 1, :] = lrecv[s]
    logs = lmat[0:NZ, :]
    share = jnp.exp2(logs - jnp.max(logs, axis=0, keepdims=True))
    lmat[0:NZ, :] = share / jnp.sum(share, axis=0, keepdims=True)
    ltr[...] = lmat[...].T
    mine = ltr[pl.ds(pl.multiple_of(lax.rem(z, 4) * ROWS, ROWS), ROWS), :]
    context = jnp.zeros((ROWS, HD), F32)
    for s in range(NZ):
        context += mine[:, s : s + 1] * crecv[s].astype(F32)

    def scatter_start(n, term):
        for f in range(NLAT):
            rsend[n, f] = term[:, f * HD : (f + 1) * HD].astype(BF16)

        def send(i, carry):
            p = in_lat(i)
            remote(rsend.at[n, p], rrecv.at[n, i], rs_sem.at[n], rr_sem.at[n], {"lat": p}).start()
            return carry

        lax.fori_loop(1, NLAT, send, 0)

    def scatter_finish(n):
        drain(rrecv.at[n, pl.ds(1, NLAT - 1)], rr_sem.at[n])
        acc = rsend[n, lme].astype(F32)
        for i in range(1, NLAT):
            acc += rrecv[n, i].astype(F32)
        return acc

    def gather_start(h):
        hsend[0] = h.astype(BF16)
        gath[lme] = h.astype(BF16)

        def send(i, carry):
            to = {"lat": in_lat(i)}
            remote(hsend.at[0], gath.at[lme], gs_sem.at[0], gr_sem.at[0], to).start()
            return carry

        lax.fori_loop(1, NLAT, send, 0)

    def gather_finish():
        drain(gath.at[pl.ds(0, NLAT - 1)], gr_sem.at[0])
        return jnp.concatenate([gath[f] for f in range(NLAT)], axis=1)

    my_cols = pl.ds(pl.multiple_of(lme * HD, HD), HD)
    scatter_start(0, dot_nn(context.astype(BF16), wov[...]))
    ring_step(0, 7)
    cross(7)
    ring_step(1, 2)
    h = basev[:, my_cols].astype(F32) + scatter_finish(0)
    gather_start(h)
    ring_step(0, 8)
    cross(8)
    ring_step(1, 3)
    drain(wbuf0.at[pl.ds(0, 31)], ws_sem.at[0])
    drain(wbuf0.at[pl.ds((1 - xh) * NZ, NZ)], wx_sem)
    rows = gather_finish()
    wide = rows.astype(F32)
    gain = lax.rsqrt(jnp.mean(wide * wide, axis=-1, keepdims=True) + 1e-06)
    qkv = (dot_nn(rows, wbuf0[:, :, : 3 * HD].reshape(D, 3 * HD)) * gain).astype(BF16)
    qx[0] = qkv[:, :HD]
    kvbuf[z] = qkv[:, HD:]

    query_out = remote(qx.at[0], qx.at[1], ps_sem.at[0], pr_sem.at[0], {"seq": partner})
    result_out = remote(sx, rx, ps_sem.at[1], pr_sem.at[1], {"seq": partner})

    def kv_move(place, i, n):
        ref = kvbuf.at[lax.rem(place, NZ)]
        return remote(ref, ref, ks_sem, kr_sem.at[n], {"seq": in_line(i)})

    for i in (4, 12, 1, 15, 2, 14, 3, 13):
        kv_move(z, i, {4: 1, 12: 2}.get(i, 0)).start()

    @pl.when(xh == 1)
    def _():
        query_out.start()

    drain(crecv.at[pl.ds(0, 15)], cs_sem)
    drain(lrecv.at[pl.ds(0, 15)], ls_sem)
    ring_step(1, 4)
    kv_move(z + 12, 4, 1).wait_recv()
    for i in range(1, 5):
        kv_move(z + 12, i, 0).start()
    kv_move(z + 4, 12, 2).wait_recv()
    for i in range(13, 16):
        kv_move(z + 4, i, 0).start()
    ring_step(1, 5)

    @pl.when(xh == 0)
    def _():
        query_out.wait_recv()

    drain(kvbuf.at[pl.ds(0, 13)], kr_sem.at[0])
    line_rows = NZ * ROWS
    raw = dot_nt(qx[...].reshape(2 * ROWS, HD), kvbuf[:, :, :HD].reshape(line_rows, HD)) * SCALE
    capped = 30.0 * jnp.tanh(raw / 30.0)
    key_row = lax.broadcasted_iota(jnp.int32, (2 * ROWS, line_rows), 1)
    row = lax.broadcasted_iota(jnp.int32, (2 * ROWS, line_rows), 0)
    seen = (key_row <= z * ROWS + row) | (row >= ROWS)
    expo = jnp.where(seen, jnp.exp(capped), 0.0)
    self_total = jnp.sum(expo, axis=1, keepdims=True)
    self_numer = dot_nn(expo.astype(BF16), kvbuf[:, :, HD:].reshape(line_rows, HD))

    @pl.when(xh == 0)
    def _():
        sx[0:ROWS, :] = self_numer[ROWS:, :]
        sx[ROWS:, :] = jnp.broadcast_to(self_total[ROWS:, :], (ROWS, HD))
        result_out.start()

    ring_step(1, 6)

    @pl.when(xh == 1)
    def _():
        result_out.wait_recv()

    self_ctx = (self_numer[0:ROWS, :] + rx[0:ROWS, :]) / (self_total[0:ROWS, :] + rx[ROWS:, :])

    home = lme // 8
    at_home = xh == home
    for f in range(NLAT):
        block = wbuf0[2 * f : 2 * f + 2, :, 3 * HD :].reshape(HD, HD)
        rsend[1, f] = dot_nt(self_ctx.astype(BF16), block).astype(BF16)
    rsend[1, lme] = (rsend[1, lme].astype(F32) + h).astype(BF16)

    def wide_send(f, carry):
        place = xh * 8 + lax.rem(f, 8)

        @pl.when(jnp.logical_or(place != lme, xh != f // 8))
        def _():
            to = {"seq": (f // 8) * NZ + z, "lat": place}
            remote(rsend.at[1, f], rrecv.at[1, lme], rs_sem.at[1], rr_sem.at[1], to).start()

        return carry

    def wide_wait(sem):
        @pl.when(at_home)
        def _():
            drain(gath.at[pl.ds(0, 15)], sem)

        @pl.when(jnp.logical_not(at_home))
        def _():
            drain(gath.at[pl.ds(0, 16)], sem)

    lax.fori_loop(0, NLAT, wide_send, 0)

    @pl.when(at_home)
    def _():
        rrecv[1, lme] = rsend[1, lme]

    ring_step(1, 7)
    wide_wait(rr_sem.at[1])
    h = rrecv[1, 0].astype(F32)
    for i in range(1, NLAT):
        h += rrecv[1, i].astype(F32)
    hsend[1] = h.astype(BF16)
    col = lax.rem(lme, 8)

    def second_send(i, carry):
        to = {"lat": in_lat(i)}
        remote(hsend.at[1], wide_in.at[home, col], gs_sem.at[1], gr_sem.at[1], to).start()
        return carry

    lax.fori_loop(1, NLAT, second_send, 0)
    wide_in[home, col] = hsend[1]
    ring_step(1, 8)
    drain(gath.at[pl.ds(0, 15)], gr_sem.at[1])
    rows = jnp.concatenate([wide_in[:, f].reshape(2 * ROWS, HD) for f in range(8)], axis=1)
    wide = rows.astype(F32)
    square = jnp.sum(wide * wide, axis=-1, keepdims=True)
    up = dot_nn(rows, wbuf1[:, 0].reshape(D // 2, HID))
    up_out[:, 0:HID] = up.astype(BF16)
    high = jnp.broadcast_to(square, (2 * ROWS, HD)).astype(BF16).astype(F32)
    lane = lax.broadcasted_iota(jnp.int32, (2 * ROWS, HD), 1)
    up_out[:, HID:] = jnp.where(lane < HD // 2, high, square - high).astype(BF16)
    half_out = remote(up_out, up_in, ps_sem.at[2], pr_sem.at[2], {"seq": partner})
    half_out.start()
    drain(wbuf1.at[pl.ds(0, 15)], ws_sem.at[1])
    drain(gath.at[pl.ds(0, 15)], rs_sem.at[0])
    wide_wait(rs_sem.at[1])
    drain(gath.at[pl.ds(0, 15)], gs_sem.at[0])
    drain(gath.at[pl.ds(0, 15)], gs_sem.at[1])
    drain(kvbuf.at[pl.ds(0, 15)], ks_sem)
    half_out.wait_recv()
    other = up_in[:, HID:].astype(F32)
    square = square + other[:, 0:1] + other[:, HD // 2 : HD // 2 + 1]
    gain = lax.rsqrt(square * (1.0 / D) + 1e-06)
    hidden = jax.nn.gelu((up + up_in[:, 0:HID].astype(F32)) * gain).astype(BF16)
    part[...] = dot_nt(hidden, wbuf1[:, 1].reshape(D // 2, HID))

    @pl.when(lme < 8)
    def _():
        cols = pl.ds(pl.multiple_of(col * HD, HD), HD)
        part[:, cols] += wide_in[:, col].reshape(2 * ROWS, HD).astype(F32)

    for p in range(2 * NLAT):
        for f in range(8):
            ftile[p, 2 * f : 2 * f + 2, :] = part[2 * p : 2 * p + 2, f * HD : (f + 1) * HD]
    fsend[...] = ftile[...].astype(BF16)
    mine = xh * NLAT + lme

    def last_send(i, carry):
        p = lax.rem(mine + i, 2 * NLAT)
        to = {"seq": (p // NLAT) * NZ + z, "lat": lax.rem(p, NLAT)}
        remote(fsend.at[p], frecv.at[mine], fs_sem, fr_sem, to).start()
        return carry

    lax.fori_loop(1, 2 * NLAT, last_send, 0)
    frecv[mine] = fsend[mine]
    half_out.wait_send()

    @pl.when(xh == 1)
    def _():
        query_out.wait_send()

    @pl.when(xh == 0)
    def _():
        result_out.wait_send()

    drain(frecv.at[pl.ds(0, 31)], fr_sem)
    for half in range(2):
        acc = frecv[half * NLAT].astype(F32)
        for i in range(1, NLAT):
            acc += frecv[half * NLAT + i].astype(F32)
        for f in range(8):
            cols = slice(half * (D // 2) + f * HD, half * (D // 2) + (f + 1) * HD)
            out_ref[:, cols] = acc[2 * f : 2 * f + 2, :].astype(BF16)
    drain(frecv.at[pl.ds(0, 31)], fs_sem)


def local(
    inputs,
    cross_kv,
    cross_out_w,
    latent_query,
    latent_base,
    latent_pos,
    attn_qkv,
    attn_out,
    mlp_up,
    mlp_down,
):
    dma = pltpu.SemaphoreType.DMA
    vmem = pl.BlockSpec(memory_space=pltpu.VMEM)
    hbm = pl.BlockSpec(memory_space=pltpu.HBM)
    return pl.pallas_call(
        kernel,
        out_shape=jax.ShapeDtypeStruct((ROWS // NLAT, D), BF16),
        in_specs=[hbm] * 10,
        out_specs=vmem,
        scratch_shapes=[
            pltpu.VMEM((TOK, D), BF16),
            pltpu.VMEM((D, 2 * HD), BF16),
            pltpu.VMEM((HD, D), BF16),
            pltpu.VMEM((ROWS, D), BF16),
            pltpu.VMEM((8, 128), jnp.int32),
            pltpu.VMEM((2, TOK, 2 * HD), BF16),
            pltpu.VMEM((NZ, ROWS, HD), BF16),
            pltpu.VMEM((NSEQ, CHUNK, HID), BF16),
            pltpu.VMEM((NZ, 2, CHUNK, HID), BF16),
            pltpu.VMEM((4, 128, 128), F32),
            pltpu.VMEM((4, 128, 128), F32),
            pltpu.VMEM((4, 128, 128), F32),
            pltpu.VMEM((NZ, ROWS, HD), BF16),
            pltpu.VMEM((NZ, ROWS, HD), BF16),
            pltpu.VMEM((4, 1, 128), F32),
            pltpu.VMEM((NZ, 1, 128), F32),
            pltpu.VMEM((128, 128), F32),
            pltpu.VMEM((128, 128), F32),
            pltpu.VMEM((2, NLAT, ROWS, HD), BF16),
            pltpu.VMEM((2, NLAT, ROWS, HD), BF16),
            pltpu.VMEM((2, ROWS, HD), BF16),
            pltpu.VMEM((NLAT, ROWS, HD), BF16),
            pltpu.VMEM((NZ, ROWS, 2 * HD), BF16),
            pltpu.VMEM((2, ROWS, HD), BF16),
            pltpu.VMEM((2 * ROWS, HD), F32),
            pltpu.VMEM((2 * ROWS, HD), F32),
            pltpu.VMEM((2, 8, ROWS, HD), BF16),
            pltpu.VMEM((2 * ROWS, HID + HD), BF16),
            pltpu.VMEM((2 * ROWS, HID + HD), BF16),
            pltpu.VMEM((2 * ROWS, D // 2), F32),
            pltpu.VMEM((2 * NLAT, 16, HD), F32),
            pltpu.VMEM((2 * NLAT, 16, HD), BF16),
            pltpu.VMEM((2 * NLAT, 16, HD), BF16),
            dma((12,)),
            dma,
            dma((4,)),
            dma,
            dma,
            dma((2,)),
            dma((2, 9)),
            dma((2, 9)),
            dma,
            dma,
            dma,
            dma,
            dma,
            dma((2,)),
            dma((2,)),
            dma((2,)),
            dma((2,)),
            dma,
            dma((3,)),
            dma((3,)),
            dma((3,)),
            dma,
            dma,
        ],
        compiler_params=pltpu.CompilerParams(
            collective_id=0, has_side_effects=True, vmem_limit_bytes=63 << 20
        ),
    )(
        inputs,
        cross_kv.reshape(D, 2 * HD),
        cross_out_w,
        latent_query,
        latent_base,
        latent_pos.reshape(8, 128),
        jnp.swapaxes(attn_qkv[0], 0, 1),
        attn_out[0],
        mlp_up[0],
        mlp_down[0],
    )


def solution(mesh):
    return jax.shard_map(
        local,
        mesh=mesh,
        in_specs=(
            P("seq", None),
            P(None, None, "lat"),
            P("lat", None),
            P("seq", "lat"),
            P("seq", None),
            P(),
            P(None, "seq", None, "lat"),
            P(None, "seq", "lat"),
            P(None, "seq", "lat"),
            P(None, "seq", "lat"),
        ),
        out_specs=P(("seq", "lat"), None),
        check_vma=False,
    )
```

```python
import math

import jax
import jax.numpy as jnp
from jax import lax
from jax.experimental import pallas as pl
from jax.experimental.pallas import tpu as pltpu
from jax.sharding import PartitionSpec as P

HD = 128
NSEQ = 32
NZ = 16
NLAT = 16
ROWS = 32
LATENTS = 1024
TOK = 768
D = 2048
HID = 512
CHUNK = 64
MESH = pl.DeviceIdType.MESH
F32 = jnp.float32
BF16 = jnp.bfloat16
LOG2E = 1.4426950408889634
SCALE = 1.0 / math.sqrt(HD)
LOW = -1e30


def dot_nt(a, b):
    return lax.dot_general(a, b, (((1,), (1,)), ((), ())), preferred_element_type=F32)


def dot_nn(a, b):
    return jnp.dot(a, b, preferred_element_type=F32)


def kernel(
    x_hbm,
    ckv_hbm,
    wo_hbm,
    q_hbm,
    base_hbm,
    pos_hbm,
    qkv_hbm,
    ow_hbm,
    up_hbm,
    down_hbm,
    out_ref,
    xv,
    ckvv,
    wov,
    basev,
    posv,
    kvt,
    qbuf,
    wbuf0,
    wbuf1,
    part_n,
    part_m,
    part_l,
    csend,
    crecv,
    lsend,
    lrecv,
    lmat,
    ltr,
    rsend,
    rrecv,
    hsend,
    gath,
    kvbuf,
    qx,
    sx,
    rx,
    wide_in,
    up_out,
    up_in,
    part,
    ftile,
    fsend,
    frecv,
    load_sem,
    qs_sem,
    qr_sem,
    xs_sem,
    xr_sem,
    ws_sem,
    wf_sem,
    wb_sem,
    wx_sem,
    cs_sem,
    cr_sem,
    ls_sem,
    lr_sem,
    rs_sem,
    rr_sem,
    gs_sem,
    gr_sem,
    ks_sem,
    kr_sem,
    ps_sem,
    pr_sem,
    fs_sem,
    fr_sem,
):
    me = lax.axis_index("seq")
    lme = lax.axis_index("lat")
    xh = me // NZ
    z = lax.rem(me, NZ)
    line = xh * NZ
    partner = lax.rem(me + NZ, NSEQ)
    my_quad = z // 4
    z_up = line + lax.rem(z + 1, NZ)
    z_down = line + lax.rem(z + NZ - 1, NZ)

    piece = TOK // 4
    pieces = [pl.ds(n * piece, piece) for n in range(4)]
    loads = [
        pltpu.make_async_copy(src, dst, load_sem.at[n])
        for n, (src, dst) in enumerate(
            (
                (ckv_hbm, ckvv),
                *((x_hbm.at[rows], xv.at[rows]) for rows in pieces),
                (q_hbm, qbuf.at[z]),
                (qkv_hbm.at[0], wbuf0.at[me, :, pl.ds(0, HD)]),
                (qkv_hbm.at[1], wbuf0.at[me, :, pl.ds(HD, HD)]),
                (qkv_hbm.at[2], wbuf0.at[me, :, pl.ds(2 * HD, HD)]),
                (ow_hbm, wbuf0.at[me, :, pl.ds(3 * HD, HD)]),
                (up_hbm, wbuf1.at[z, 0]),
                (down_hbm, wbuf1.at[z, 1]),
                (pos_hbm, posv),
                (wo_hbm, wov),
                (base_hbm, basev),
            )
        )
    ]
    for load in loads:
        load.start()

    barrier = pltpu.get_barrier_semaphore()

    def greet(device_id):
        pl.semaphore_signal(barrier, inc=1, device_id=device_id, device_id_type=MESH)

    def in_line(i):
        return line + lax.rem(z + i, NZ)

    def in_lat(i):
        return lax.rem(lme + i, NLAT)

    def greet_all(i, carry):
        greet({"seq": in_line(i)})
        greet({"lat": in_lat(i)})
        greet({"seq": partner, "lat": in_lat(i)})
        return carry

    lax.fori_loop(1, NZ, greet_all, 0)
    qx[1] = jnp.zeros((ROWS, HD), BF16)
    rx[...] = jnp.zeros_like(rx)
    greet({"seq": partner})
    loads[5].wait()
    pl.semaphore_wait(barrier, NZ - 1 + 1 + 2 * (NLAT - 1))

    def drain(ref, sem):
        pltpu.make_async_copy(ref, ref, sem).wait()

    def remote(src, dst, send_sem, recv_sem, device_id):
        return pltpu.make_async_remote_copy(
            src_ref=src,
            dst_ref=dst,
            send_sem=send_sem,
            recv_sem=recv_sem,
            device_id=device_id,
            device_id_type=MESH,
        )

    def send_query(n, carry):
        i = 8 + (1 - 2 * lax.rem(n, 2)) * (n // 2)
        remote(qbuf.at[z], qbuf.at[z], qs_sem, qr_sem.at[my_quad], {"seq": in_line(i)}).start()
        return carry

    lax.fori_loop(1, NZ, send_query, 0)

    def chunk(r, place):
        return wbuf0.at[line + place] if r == 0 else wbuf1.at[place]

    def move(r, place, to, recv_sem):
        ref = chunk(r, place)
        return remote(ref, ref, ws_sem.at[r], recv_sem, {"seq": to})

    def ring_start(r):
        move(r, z, z_up, wf_sem.at[r, 1]).start()
        move(r, z, z_down, wb_sem.at[r, 1]).start()

    def ring_step(r, k):
        low = lax.rem(z + NZ - k, NZ)
        high = lax.rem(z + k, NZ)
        move(r, low, z_up, wf_sem.at[r, k]).wait_recv()
        if k < 8:
            move(r, low, z_up, wf_sem.at[r, k + 1]).start()
            move(r, high, z_down, wb_sem.at[r, k]).wait_recv()
            if k < 7:
                move(r, high, z_down, wb_sem.at[r, k + 1]).start()

    def cross(k):
        move(0, lax.rem(z + NZ - k, NZ), partner, wx_sem).start()
        if 0 < k < 8:
            move(0, lax.rem(z + k, NZ), partner, wx_sem).start()

    loads[0].wait()
    for n, rows in enumerate(pieces):
        loads[1 + n].wait()
        kvt[0, rows, :] = dot_nn(xv[rows, :], ckvv[...]).astype(BF16)
        remote(kvt.at[0, rows], kvt.at[1, rows], xs_sem, xr_sem, {"seq": partner}).start()
        if n == 0:
            for load in loads[6:10]:
                load.wait()
            ring_start(0)
    for load in loads[10:]:
        load.wait()
    ring_step(0, 1)

    def attend(quad, slot, owner):
        q = qbuf[pl.ds(quad * 4, 4)].reshape(4 * ROWS, HD)
        scores = dot_nt(q, kvt[slot, :, :HD])
        row = posv[pl.ds(xh * 4 + quad, 1), :].astype(F32)
        pos = jnp.broadcast_to(row, (128, 128)).T[:, 0:1]
        key = lax.broadcasted_iota(jnp.int32, (1, TOK), 1) + owner * TOK
        allowed = key.astype(F32) <= pos
        top = jnp.max(jnp.where(allowed, scores, LOW), axis=1, keepdims=True)
        weights = jnp.where(allowed, jnp.exp2((scores - top) * (SCALE * LOG2E)), 0.0)
        total = jnp.sum(weights, axis=1, keepdims=True)
        numer = dot_nn(weights.astype(BF16), kvt[slot, :, HD:])
        return top, total, numer

    def first_pass(j, carry):
        quad = lax.rem(my_quad + j, 4)

        @pl.when(j == 0)
        def _():
            drain(qbuf.at[pl.ds(0, 3)], qr_sem.at[quad])

        @pl.when(j > 0)
        def _():
            drain(qbuf.at[pl.ds(0, 4)], qr_sem.at[quad])

        top, total, numer = attend(quad, 0, me)
        part_n[quad] = numer
        part_m[quad] = jnp.broadcast_to(top, (128, 128))
        part_l[quad] = jnp.broadcast_to(total, (128, 128))
        return carry

    def second_pass(j, carry):
        quad = lax.rem(my_quad + 1 + j, 4)
        top, total, numer = attend(quad, 1, partner)
        top_1 = part_m[quad]
        best = jnp.maximum(top_1, top)
        left = jnp.exp2((top_1 - best) * (SCALE * LOG2E))
        right = jnp.exp2((top - best) * (SCALE * LOG2E))
        total = part_l[quad] * left + total * right
        some = total > 0.0
        safe = jnp.where(some, total, 1.0)
        ctx = (part_n[quad] * left + numer * right) / safe
        lse = jnp.where(some, best * (SCALE * LOG2E) + jnp.log2(safe), LOW)
        csend[pl.ds(quad * 4, 4)] = ctx.astype(BF16).reshape(4, ROWS, HD)
        lsend[quad] = lse.T[0:1, :]

        def send_part(t, carry):
            p = quad * 4 + t

            @pl.when(p != z)
            def _():
                to = {"seq": line + p}
                remote(csend.at[p], crecv.at[z], cs_sem, cr_sem, to).start()
                remote(lsend.at[quad], lrecv.at[z], ls_sem, lr_sem, to).start()

            return carry

        lax.fori_loop(0, 4, send_part, 0)
        return carry

    lax.fori_loop(0, 2, first_pass, 0)
    ring_step(0, 2)
    lax.fori_loop(2, 4, first_pass, 0)
    drain(kvt.at[1], xr_sem)
    ring_step(0, 3)
    lax.fori_loop(0, 4, second_pass, 0)
    ring_step(0, 4)
    ring_start(1)
    for k in range(5):
        cross(k)
    crecv[z] = csend[z]
    lrecv[z] = lsend[my_quad]
    drain(qbuf.at[pl.ds(0, 15)], qs_sem)
    drain(kvt.at[0], xs_sem)
    ring_step(0, 5)
    cross(5)
    ring_step(1, 1)
    ring_step(0, 6)
    cross(6)
    drain(crecv.at[pl.ds(0, 15)], cr_sem)
    drain(lrecv.at[pl.ds(0, 15)], lr_sem)

    lmat[...] = jnp.zeros((128, 128), F32)
    for s in range(NZ):
        lmat[s : s + 1, :] = lrecv[s]
    logs = lmat[0:NZ, :]
    share = jnp.exp2(logs - jnp.max(logs, axis=0, keepdims=True))
    lmat[0:NZ, :] = share / jnp.sum(share, axis=0, keepdims=True)
    ltr[...] = lmat[...].T
    mine = ltr[pl.ds(pl.multiple_of(lax.rem(z, 4) * ROWS, ROWS), ROWS), :]
    context = jnp.zeros((ROWS, HD), F32)
    for s in range(NZ):
        context += mine[:, s : s + 1] * crecv[s].astype(F32)

    def scatter_start(n, term):
        for f in range(NLAT):
            rsend[n, f] = term[:, f * HD : (f + 1) * HD].astype(BF16)

        def send(i, carry):
            p = in_lat(i)
            remote(rsend.at[n, p], rrecv.at[n, i], rs_sem.at[n], rr_sem.at[n], {"lat": p}).start()
            return carry

        lax.fori_loop(1, NLAT, send, 0)

    def scatter_finish(n):
        drain(rrecv.at[n, pl.ds(1, NLAT - 1)], rr_sem.at[n])
        acc = rsend[n, lme].astype(F32)
        for i in range(1, NLAT):
            acc += rrecv[n, i].astype(F32)
        return acc

    def gather_start(h):
        hsend[0] = h.astype(BF16)
        gath[lme] = h.astype(BF16)

        def send(i, carry):
            to = {"lat": in_lat(i)}
            remote(hsend.at[0], gath.at[lme], gs_sem.at[0], gr_sem.at[0], to).start()
            return carry

        lax.fori_loop(1, NLAT, send, 0)

    def gather_finish():
        drain(gath.at[pl.ds(0, NLAT - 1)], gr_sem.at[0])
        return jnp.concatenate([gath[f] for f in range(NLAT)], axis=1)

    my_cols = pl.ds(pl.multiple_of(lme * HD, HD), HD)
    scatter_start(0, dot_nn(context.astype(BF16), wov[...]))
    ring_step(0, 7)
    cross(7)
    ring_step(1, 2)
    h = basev[:, my_cols].astype(F32) + scatter_finish(0)
    gather_start(h)
    ring_step(0, 8)
    cross(8)
    ring_step(1, 3)
    drain(wbuf0.at[pl.ds(0, 31)], ws_sem.at[0])
    drain(wbuf0.at[pl.ds((1 - xh) * NZ, NZ)], wx_sem)
    rows = gather_finish()
    wide = rows.astype(F32)
    gain = lax.rsqrt(jnp.mean(wide * wide, axis=-1, keepdims=True) + 1e-06)
    qkv = (dot_nn(rows, wbuf0[:, :, : 3 * HD].reshape(D, 3 * HD)) * gain).astype(BF16)
    qx[0] = qkv[:, :HD]
    kvbuf[z] = qkv[:, HD:]

    query_out = remote(qx.at[0], qx.at[1], ps_sem.at[0], pr_sem.at[0], {"seq": partner})
    result_out = remote(sx, rx, ps_sem.at[1], pr_sem.at[1], {"seq": partner})

    def kv_move(place, i, n):
        ref = kvbuf.at[lax.rem(place, NZ)]
        return remote(ref, ref, ks_sem, kr_sem.at[n], {"seq": in_line(i)})

    for i in (4, 12, 1, 15, 2, 14, 3, 13):
        kv_move(z, i, {4: 1, 12: 2}.get(i, 0)).start()

    @pl.when(xh == 1)
    def _():
        query_out.start()

    drain(crecv.at[pl.ds(0, 15)], cs_sem)
    drain(lrecv.at[pl.ds(0, 15)], ls_sem)
    ring_step(1, 4)
    kv_move(z + 12, 4, 1).wait_recv()
    for i in range(1, 5):
        kv_move(z + 12, i, 0).start()
    kv_move(z + 4, 12, 2).wait_recv()
    for i in range(13, 16):
        kv_move(z + 4, i, 0).start()
    ring_step(1, 5)

    @pl.when(xh == 0)
    def _():
        query_out.wait_recv()

    drain(kvbuf.at[pl.ds(0, 13)], kr_sem.at[0])
    line_rows = NZ * ROWS
    raw = dot_nt(qx[...].reshape(2 * ROWS, HD), kvbuf[:, :, :HD].reshape(line_rows, HD)) * SCALE
    capped = 30.0 * jnp.tanh(raw / 30.0)
    key_row = lax.broadcasted_iota(jnp.int32, (2 * ROWS, line_rows), 1)
    row = lax.broadcasted_iota(jnp.int32, (2 * ROWS, line_rows), 0)
    seen = (key_row <= z * ROWS + row) | (row >= ROWS)
    expo = jnp.where(seen, jnp.exp(capped), 0.0)
    self_total = jnp.sum(expo, axis=1, keepdims=True)
    self_numer = dot_nn(expo.astype(BF16), kvbuf[:, :, HD:].reshape(line_rows, HD))

    @pl.when(xh == 0)
    def _():
        sx[0:ROWS, :] = self_numer[ROWS:, :]
        sx[ROWS:, :] = jnp.broadcast_to(self_total[ROWS:, :], (ROWS, HD))
        result_out.start()

    ring_step(1, 6)

    @pl.when(xh == 1)
    def _():
        result_out.wait_recv()

    self_ctx = (self_numer[0:ROWS, :] + rx[0:ROWS, :]) / (self_total[0:ROWS, :] + rx[ROWS:, :])

    home = lme // 8
    at_home = xh == home
    for f in range(NLAT):
        block = wbuf0[2 * f : 2 * f + 2, :, 3 * HD :].reshape(HD, HD)
        rsend[1, f] = dot_nt(self_ctx.astype(BF16), block).astype(BF16)
    rsend[1, lme] = (rsend[1, lme].astype(F32) + h).astype(BF16)

    def wide_send(f, carry):
        place = xh * 8 + lax.rem(f, 8)

        @pl.when(jnp.logical_or(place != lme, xh != f // 8))
        def _():
            to = {"seq": (f // 8) * NZ + z, "lat": place}
            remote(rsend.at[1, f], rrecv.at[1, lme], rs_sem.at[1], rr_sem.at[1], to).start()

        return carry

    def wide_wait(sem):
        @pl.when(at_home)
        def _():
            drain(gath.at[pl.ds(0, 15)], sem)

        @pl.when(jnp.logical_not(at_home))
        def _():
            drain(gath.at[pl.ds(0, 16)], sem)

    lax.fori_loop(0, NLAT, wide_send, 0)

    @pl.when(at_home)
    def _():
        rrecv[1, lme] = rsend[1, lme]

    ring_step(1, 7)
    wide_wait(rr_sem.at[1])
    h = rrecv[1, 0].astype(F32)
    for i in range(1, NLAT):
        h += rrecv[1, i].astype(F32)
    hsend[1] = h.astype(BF16)
    col = lax.rem(lme, 8)

    def second_send(i, carry):
        to = {"lat": in_lat(i)}
        remote(hsend.at[1], wide_in.at[home, col], gs_sem.at[1], gr_sem.at[1], to).start()
        return carry

    lax.fori_loop(1, NLAT, second_send, 0)
    wide_in[home, col] = hsend[1]
    ring_step(1, 8)
    drain(gath.at[pl.ds(0, 15)], gr_sem.at[1])
    rows = jnp.concatenate([wide_in[:, f].reshape(2 * ROWS, HD) for f in range(8)], axis=1)
    wide = rows.astype(F32)
    square = jnp.sum(wide * wide, axis=-1, keepdims=True)
    up = dot_nn(rows, wbuf1[:, 0].reshape(D // 2, HID))
    up_out[:, 0:HID] = up.astype(BF16)
    high = jnp.broadcast_to(square, (2 * ROWS, HD)).astype(BF16).astype(F32)
    lane = lax.broadcasted_iota(jnp.int32, (2 * ROWS, HD), 1)
    up_out[:, HID:] = jnp.where(lane < HD // 2, high, square - high).astype(BF16)
    half_out = remote(up_out, up_in, ps_sem.at[2], pr_sem.at[2], {"seq": partner})
    half_out.start()
    drain(wbuf1.at[pl.ds(0, 15)], ws_sem.at[1])
    drain(gath.at[pl.ds(0, 15)], rs_sem.at[0])
    wide_wait(rs_sem.at[1])
    drain(gath.at[pl.ds(0, 15)], gs_sem.at[0])
    drain(gath.at[pl.ds(0, 15)], gs_sem.at[1])
    drain(kvbuf.at[pl.ds(0, 15)], ks_sem)
    half_out.wait_recv()
    other = up_in[:, HID:].astype(F32)
    square = square + other[:, 0:1] + other[:, HD // 2 : HD // 2 + 1]
    gain = lax.rsqrt(square * (1.0 / D) + 1e-06)
    hidden = jax.nn.gelu((up + up_in[:, 0:HID].astype(F32)) * gain).astype(BF16)
    part[...] = dot_nt(hidden, wbuf1[:, 1].reshape(D // 2, HID))

    @pl.when(lme < 8)
    def _():
        cols = pl.ds(pl.multiple_of(col * HD, HD), HD)
        part[:, cols] += wide_in[:, col].reshape(2 * ROWS, HD).astype(F32)

    for p in range(2 * NLAT):
        for f in range(8):
            ftile[p, 2 * f : 2 * f + 2, :] = part[2 * p : 2 * p + 2, f * HD : (f + 1) * HD]
    fsend[...] = ftile[...].astype(BF16)
    mine = xh * NLAT + lme

    def last_send(i, carry):
        p = lax.rem(mine + i, 2 * NLAT)
        to = {"seq": (p // NLAT) * NZ + z, "lat": lax.rem(p, NLAT)}
        remote(fsend.at[p], frecv.at[mine], fs_sem, fr_sem, to).start()
        return carry

    lax.fori_loop(1, 2 * NLAT, last_send, 0)
    frecv[mine] = fsend[mine]
    half_out.wait_send()

    @pl.when(xh == 1)
    def _():
        query_out.wait_send()

    @pl.when(xh == 0)
    def _():
        result_out.wait_send()

    drain(frecv.at[pl.ds(0, 31)], fr_sem)
    for half in range(2):
        acc = frecv[half * NLAT].astype(F32)
        for i in range(1, NLAT):
            acc += frecv[half * NLAT + i].astype(F32)
        for f in range(8):
            cols = slice(half * (D // 2) + f * HD, half * (D // 2) + (f + 1) * HD)
            out_ref[:, cols] = acc[2 * f : 2 * f + 2, :].astype(BF16)
    drain(frecv.at[pl.ds(0, 31)], fs_sem)


def local(
    inputs,
    cross_kv,
    cross_out_w,
    latent_query,
    latent_base,
    latent_pos,
    attn_qkv,
    attn_out,
    mlp_up,
    mlp_down,
):
    dma = pltpu.SemaphoreType.DMA
    vmem = pl.BlockSpec(memory_space=pltpu.VMEM)
    hbm = pl.BlockSpec(memory_space=pltpu.HBM)
    return pl.pallas_call(
        kernel,
        out_shape=jax.ShapeDtypeStruct((ROWS // NLAT, D), BF16),
        in_specs=[hbm] * 10,
        out_specs=vmem,
        scratch_shapes=[
            pltpu.VMEM((TOK, D), BF16),
            pltpu.VMEM((D, 2 * HD), BF16),
            pltpu.VMEM((HD, D), BF16),
            pltpu.VMEM((ROWS, D), BF16),
            pltpu.VMEM((8, 128), jnp.int32),
            pltpu.VMEM((2, TOK, 2 * HD), BF16),
            pltpu.VMEM((NZ, ROWS, HD), BF16),
            pltpu.VMEM((NSEQ, CHUNK, HID), BF16),
            pltpu.VMEM((NZ, 2, CHUNK, HID), BF16),
            pltpu.VMEM((4, 128, 128), F32),
            pltpu.VMEM((4, 128, 128), F32),
            pltpu.VMEM((4, 128, 128), F32),
            pltpu.VMEM((NZ, ROWS, HD), BF16),
            pltpu.VMEM((NZ, ROWS, HD), BF16),
            pltpu.VMEM((4, 1, 128), F32),
            pltpu.VMEM((NZ, 1, 128), F32),
            pltpu.VMEM((128, 128), F32),
            pltpu.VMEM((128, 128), F32),
            pltpu.VMEM((2, NLAT, ROWS, HD), BF16),
            pltpu.VMEM((2, NLAT, ROWS, HD), BF16),
            pltpu.VMEM((2, ROWS, HD), BF16),
            pltpu.VMEM((NLAT, ROWS, HD), BF16),
            pltpu.VMEM((NZ, ROWS, 2 * HD), BF16),
            pltpu.VMEM((2, ROWS, HD), BF16),
            pltpu.VMEM((2 * ROWS, HD), F32),
            pltpu.VMEM((2 * ROWS, HD), F32),
            pltpu.VMEM((2, 8, ROWS, HD), BF16),
            pltpu.VMEM((2 * ROWS, HID + HD), BF16),
            pltpu.VMEM((2 * ROWS, HID + HD), BF16),
            pltpu.VMEM((2 * ROWS, D // 2), F32),
            pltpu.VMEM((2 * NLAT, 16, HD), F32),
            pltpu.VMEM((2 * NLAT, 16, HD), BF16),
            pltpu.VMEM((2 * NLAT, 16, HD), BF16),
            dma((15,)),
            dma,
            dma((4,)),
            dma,
            dma,
            dma((2,)),
            dma((2, 9)),
            dma((2, 9)),
            dma,
            dma,
            dma,
            dma,
            dma,
            dma((2,)),
            dma((2,)),
            dma((2,)),
            dma((2,)),
            dma,
            dma((3,)),
            dma((3,)),
            dma((3,)),
            dma,
            dma,
        ],
        compiler_params=pltpu.CompilerParams(
            collective_id=0, has_side_effects=True, vmem_limit_bytes=63 << 20
        ),
    )(
        inputs,
        cross_kv.reshape(D, 2 * HD),
        cross_out_w,
        latent_query,
        latent_base,
        latent_pos.reshape(8, 128),
        jnp.swapaxes(attn_qkv[0], 0, 1),
        attn_out[0],
        mlp_up[0],
        mlp_down[0],
    )


def solution(mesh):
    return jax.shard_map(
        local,
        mesh=mesh,
        in_specs=(
            P("seq", None),
            P(None, None, "lat"),
            P("lat", None),
            P("seq", "lat"),
            P("seq", None),
            P(),
            P(None, "seq", None, "lat"),
            P(None, "seq", "lat"),
            P(None, "seq", "lat"),
            P(None, "seq", "lat"),
        ),
        out_specs=P(("seq", "lat"), None),
        check_vma=False,
    )
```
